32 devices in a mesh: chain: 2 (over x), slab: 16 (over z, y, core).
Axes of the slice: x: 2, y: 2, z: 4, core: 2. Of those that a mesh axis runs over, the one named last changes fastest.
Arguments:
- whitened: float32 [1024, 256, 256], P(('chain', 'slab')), parts along dimension 0, may hold values from -6 to 6
- counts: int32 [1024, 256, 256], P(('chain', 'slab')), parts along dimension 0, may hold values from 0 to 24
- exposure: int32 [1024, 256, 256], P(('chain', 'slab')), parts along dimension 0, may hold values from 1 to 12
- cholesky_east: float32 [512, 512], replicated, as said below
- cholesky_north: float32 [256, 256], replicated, as said below
- cholesky_time: float32 [256, 256], replicated, as said below
Outputs:
- gradient: float32 [1024, 256, 256], P(('chain', 'slab')), parts along dimension 0
- density: float32 [2], P('chain'), parts along dimension 0
The draws below stay inside these ranges and needn't reach their ends.
There are 2 independent parts, one for each index of `chain`. The reference program is written for one: setup_inputs(seed, part) draws one part's arguments, and reference() takes and returns one part's arrays. A program takes and returns all parts, laid end to end along the dimension named above; an argument that names none is the same for every part. Nothing has to cross between parts.
Inputs may be any that keep to these rules, and one draw needn't show every extreme that they name: `cholesky_east`: lower triangular with a positive diagonal, each row of unit length. `cholesky_north`: lower triangular with a positive diagonal, each row of unit length. `cholesky_time`: lower triangular with a positive diagonal, each row of unit length.
All inputs are finite; a program needn't handle non-finite values.
Results may differ from the reference program's by a relative error of at most 0.00008.
Values sent between devices are 32-bit elements; how exact they have to be, the bound alone decides.
No kernel may reach another device: no remote copies, remote signals or barrier semaphores. Data moves between devices by JAX's collectives and lax.ppermute only.
A program may use at most 128 MiB of HBM per device.

```python
import jax
import jax.numpy as jnp
from jax import lax

NX = 512
NY = 256
NT = 256


def lower_factor(key, extent):
    key_off, key_diag = jax.random.split(key)
    random_part = jax.random.normal(key_off, (extent, extent), jnp.float32)
    row_index = lax.broadcasted_iota(jnp.int32, (extent, extent), 0)
    col_index = lax.broadcasted_iota(jnp.int32, (extent, extent), 1)
    spread = 0.6
    lower_part = jnp.where(col_index < row_index, random_part * spread / jnp.sqrt(row_index.astype(jnp.float32) + 1.0), 0.0)
    diagonal = jax.random.uniform(key_diag, (extent,), jnp.float32, 0.7, 1.3)
    lower_part = lower_part + jnp.diag(diagonal)
    return lower_part / jnp.sqrt(jnp.sum(lower_part * lower_part, axis=1, keepdims=True))


def draw_cholesky_east(key, part):
    return lower_factor(jax.random.fold_in(key, 101), NX)


def draw_cholesky_north(key, part):
    return lower_factor(jax.random.fold_in(key, 202), NY)


def draw_cholesky_time(key, part):
    return lower_factor(jax.random.fold_in(key, 303), NT)


def observed_pair(key):
    base_key = jax.random.fold_in(key, 404)
    key_exposure, key_counts = jax.random.split(base_key)
    east_index = lax.broadcasted_iota(jnp.int32, (NX, NY, NT), 0)
    exposure = jax.random.randint(key_exposure, (NX, NY, NT), 1, 5, dtype=jnp.int32) + 8 * east_index // NX
    counts = jax.random.randint(key_counts, (NX, NY, NT), 0, 2 * exposure + 1, dtype=jnp.int32)
    return (counts, exposure)


def draw_counts(key, part):
    return observed_pair(key)[0]


def draw_exposure(key, part):
    return observed_pair(key)[1]


def block_scale(rng, shape, cuts, low, top_value):
    level, own = 1.0, jax.random.fold_in(rng, 6)
    for axis_at, shards_of in cuts:
        draws = jnp.exp(jax.random.uniform(jax.random.fold_in(own, axis_at), (shards_of,), jnp.float32, low / len(cuts), top_value / len(cuts)))
        level = level * jnp.repeat(draws, shape[axis_at] // shards_of).reshape([-1 if axis == axis_at else 1 for axis in range(len(shape))])
    return level


def bell_draw(stream_key, dims, scale, limit, pieces=(), held_as=jnp.bfloat16):
    loudness = block_scale(stream_key, dims, pieces, -0.22, 0.18) if pieces else 1.0
    entries = jax.random.normal(stream_key, dims, jnp.float32) * scale * loudness
    return jnp.minimum(jnp.maximum(entries, -limit), limit).astype(held_as)


def setup_inputs(seed: int = 0, part: int = 0) -> dict:
    key_of = jax.random.split(jax.random.key(seed), 7)
    own_keys = jax.random.split(jax.random.fold_in(key_of[6], part), 7)
    whitened = bell_draw(own_keys[0], (NX, NY, NT), 1.0, 6.0, ((0, 16),), jnp.float32)
    counts = draw_counts(jax.random.fold_in(jax.random.fold_in(key_of[6], part), 71), part)
    exposure = draw_exposure(jax.random.fold_in(jax.random.fold_in(key_of[6], part), 71), part)
    cholesky_east = draw_cholesky_east(jax.random.fold_in(key_of[6], 71), part)
    cholesky_north = draw_cholesky_north(jax.random.fold_in(key_of[6], 71), part)
    cholesky_time = draw_cholesky_time(jax.random.fold_in(key_of[6], 71), part)
    return dict(whitened=whitened, counts=counts, exposure=exposure, cholesky_east=cholesky_east, cholesky_north=cholesky_north, cholesky_time=cholesky_time)


field_scale = 0.6


def mode_last(values, matrix):
    return jnp.einsum("abc,tc->abt", values, matrix, precision=lax.Precision.HIGHEST)


def mode_middle(values, matrix):
    return jnp.einsum("abc,yb->ayc", values, matrix, precision=lax.Precision.HIGHEST)


def mode_first(values, matrix):
    return jnp.einsum("abc,xa->xbc", values, matrix, precision=lax.Precision.HIGHEST)


def adjoint_last(values, matrix):
    return jnp.einsum("abt,tc->abc", values, matrix, precision=lax.Precision.HIGHEST)


def adjoint_middle(values, matrix):
    return jnp.einsum("ayc,yb->abc", values, matrix, precision=lax.Precision.HIGHEST)


def adjoint_first(values, matrix):
    return jnp.einsum("xbc,xa->abc", values, matrix, precision=lax.Precision.HIGHEST)


def reference(whitened, counts, exposure, cholesky_east, cholesky_north, cholesky_time):
    values = mode_first(mode_middle(mode_last(whitened, cholesky_time), cholesky_north), cholesky_east)
    log_rate = field_scale * values
    observed = counts.astype(jnp.float32)
    intensity = exposure.astype(jnp.float32) * jnp.exp(log_rate)
    residual = observed - intensity
    total_sum = jnp.sum(observed * log_rate - intensity) - 0.5 * jnp.sum(whitened * whitened)
    density = total_sum / (NX * NY * NT)
    adjoint = adjoint_last(adjoint_middle(adjoint_first(residual, cholesky_east), cholesky_north), cholesky_time)
    gradient = field_scale * adjoint - whitened
    return gradient, jnp.reshape(density, (1,))
```

```python
import functools

import jax
import jax.numpy as jnp
from jax import lax
from jax.experimental import pallas as pl
from jax.experimental.pallas import tpu as pltpu
from jax.sharding import PartitionSpec as P

field_scale = 0.6
layers = 4
chunk_target = 16
lanes = 128
f32, bf16 = jnp.float32, jnp.bfloat16
ANY = pl.BlockSpec(memory_space=pl.ANY)
SMEM = pl.BlockSpec(memory_space=pltpu.SMEM)
params = functools.partial(pltpu.CompilerParams, vmem_limit_bytes=48 * 1024 * 1024)


def split(values):
    high = values.astype(bf16)
    return high, (values - high.astype(f32)).astype(bf16)


def dot(left, right):
    return jnp.dot(left, right, preferred_element_type=f32)


def product(left, right):
    return dot(left[0], right[0]) + (dot(left[0], right[1]) + dot(left[1], right[0]))


def whole(shape):
    return pl.BlockSpec(shape, lambda *_: (0,) * len(shape))


def cost(flops, transferred):
    return pl.CostEstimate(flops=int(flops), bytes_accessed=int(transferred), transcendentals=0)


def fold_rows(values):
    return jnp.sum(values.reshape(-1, 8, values.shape[-1]), axis=0)


def permuted_rows(matrix, bounds, peers):
    rows = matrix.shape[0] // peers
    return jnp.concatenate([matrix[q * rows + low : q * rows + high] for low, high in bounds for q in range(peers)], axis=0)


def field_factors(cholesky_north, cholesky_time, bounds, peers):
    def kernel(north, time, north_high, north_low, time_high, time_low):
        north_high[...], north_low[...] = split(permuted_rows(north[...], bounds, peers))
        time_high[...], time_low[...] = split(time[...].T)

    ny, nt = cholesky_north.shape[0], cholesky_time.shape[0]
    pair = lambda size: [jax.ShapeDtypeStruct((size, size), bf16)] * 2
    return pl.pallas_call(kernel, out_shape=pair(ny) + pair(nt), compiler_params=params(), name="field_factors")(cholesky_north, cholesky_time)


def other_factors(layer, cholesky_east, cholesky_north, cholesky_time, bounds, peers, held_back):
    nx = cholesky_east.shape[0]
    span, half = nx // layers, nx // 2

    def kernel(layer_ref, east, north, time, _, *outs):
        def put(place, values):
            outs[2 * place][...], outs[2 * place + 1][...] = split(values)

        here = layer_ref[0]
        put(0, permuted_rows(north[...], bounds, peers).T)
        put(1, time[...])

        @pl.when(here == 1)
        def _():
            put(2, field_scale * east[half:, :half])

        @pl.when(here != 1)
        def _():
            cross = (field_scale * east[half:, :half]).T
            put(2, jnp.concatenate([cross[span:], cross[:span]], axis=0))

        for z in range(layers):

            @pl.when(here == z)
            def _(z=z):
                own = field_scale * east[z * span : (z + 1) * span, z * span : (z + 1) * span]
                put(3, own)
                put(4, own.T)
                if z % 2:
                    put(5, field_scale * east[z * span : (z + 1) * span, (z - 1) * span : z * span])
                else:
                    put(5, (field_scale * east[(z + 1) * span : (z + 2) * span, z * span : (z + 1) * span]).T)

    ny, nt = cholesky_north.shape[0], cholesky_time.shape[0]
    sizes = (ny, nt, half, span, span, span)
    shapes = [jax.ShapeDtypeStruct((size, size), bf16) for size in sizes for _ in range(2)]
    outs = pl.pallas_call(
        kernel,
        out_shape=shapes,
        in_specs=[SMEM, whole((nx, nx)), whole((ny, ny)), whole((nt, nt)), ANY],
        out_specs=[whole(s.shape) for s in shapes],
        grid=(1,),
        compiler_params=params(),
        name="other_factors",
    )(layer, cholesky_east, cholesky_north, cholesky_time, held_back)
    return [tuple(outs[2 * i : 2 * i + 2]) for i in range(len(sizes))]


def field(whitened, factors, bounds, peers):
    planes, ny, nt = whitened.shape
    step = 8
    counts = [peers * (high - low) for low, high in bounds]
    parts = nt // lanes

    def kernel(w, north_high, north_low, time_high, time_low, *outs):
        squares = outs[-1]
        north = (north_high[...], north_low[...])
        time = (time_high[...], time_low[...])

        @pl.when(pl.program_id(0) == 0)
        def _():
            squares[...] = jnp.zeros_like(squares)

        def one(x, total):
            values = w[x]
            mixed = product(north, split(product(split(values), time)))
            start = 0
            for out, rows in zip(outs[:-1], counts):
                for h in range(parts):
                    out.reshape(rows * parts * step, lanes)[pl.ds(h * step + x, rows, stride=parts * step), :] = mixed[
                        start : start + rows, h * lanes : (h + 1) * lanes
                    ]
                start += rows
            return total + fold_rows(values * values)

        squares[...] += lax.fori_loop(0, step, one, jnp.zeros((8, nt), f32), unroll=2)

    *groups, squares = pl.pallas_call(
        kernel,
        grid=(planes // step,),
        in_specs=[pl.BlockSpec((step, ny, nt), lambda i: (i, 0, 0))] + [whole(f.shape) for f in factors],
        out_specs=[pl.BlockSpec((rows, parts, step, lanes), lambda i: (0, 0, i, 0)) for rows in counts] + [whole((8, nt))],
        out_shape=[jax.ShapeDtypeStruct((rows, parts, planes, lanes), f32) for rows in counts] + [jax.ShapeDtypeStruct((8, nt), f32)],
        compiler_params=params(),
        cost_estimate=cost(12 * planes * ny * nt * nt, 8 * whitened.size),
        name="field",
    )(whitened, *factors)
    return [g.reshape(peers, -1, *g.shape[1:]) for g in groups], squares


def packed(counts, exposure, low, high, peers, held_back):
    planes, ny, nt = counts.shape
    rows, parts = high - low, nt // lanes
    band = 8 if rows % 8 == 0 and low % 8 == 0 and (ny // peers) % 8 == 0 else rows
    per_peer = ny // peers // band

    def kernel(c, e, _, out):
        for h in range(parts):
            out[0, 0, h] = c[:, :, h * lanes : (h + 1) * lanes].astype(f32)
            out[0, 1, h] = e[:, :, h * lanes : (h + 1) * lanes].astype(f32)

    source = pl.BlockSpec((planes, band, nt), lambda q, j: (0, q * per_peer + low // band + j, 0))
    return pl.pallas_call(
        kernel,
        grid=(peers, rows // band),
        in_specs=[source, source, ANY],
        out_specs=pl.BlockSpec((1, 2, parts, planes, band, lanes), lambda q, j: (q, 0, 0, 0, j, 0)),
        out_shape=jax.ShapeDtypeStruct((peers, 2, parts, planes, rows, lanes), f32),
        compiler_params=params(),
        cost_estimate=cost(0, 16 * peers * planes * rows * nt),
        name="packed",
    )(counts, exposure, held_back)


def gate(values, held_back):
    def kernel(_, __, out):
        pass

    return pl.pallas_call(
        kernel,
        in_specs=[ANY, ANY],
        out_specs=ANY,
        out_shape=jax.ShapeDtypeStruct(values.shape, values.dtype),
        input_output_aliases={0: 0},
        name="gate",
    )(values, held_back)


def lines(block):
    peers, _, parts = block.shape[:3]
    return jnp.concatenate([jnp.concatenate([block[q, 0, h] for h in range(parts)], axis=1) for q in range(peers)], axis=0)


def put_lines(out, values):
    peers, _, parts, planes, width = out.shape
    for q in range(peers):
        for h in range(parts):
            out[q, 0, h] = values[q * planes : (q + 1) * planes, h * width : (h + 1) * width]


def rows_of(array, start):
    peers, _, *rest = array.shape
    return pl.BlockSpec((peers, 1, *rest), lambda y: (0, start + y, 0, 0, 0))


def cross_terms(layer, cross, crossed, own_field, own_residual, rows):
    operands, specs = [layer, *cross, crossed], [SMEM, whole(cross[0].shape), whole(cross[1].shape), rows_of(crossed, 0)]
    for pair in (own_field, own_residual):
        if pair is not None:
            operands.append(pair[0])
            specs.append(rows_of(*pair))
    peers, _, parts, planes, _ = crossed.shape
    span, nt = peers * planes, parts * lanes

    def kernel(layer_ref, high, low, moved, *rest):
        near, far = rest[-2:]
        rest = list(rest[:-2])
        here = layer_ref[0]

        def run(first, second):
            result = product((high[...], low[...]), split(jnp.concatenate([lines(first), lines(second)], axis=0)))
            put_lines(near, result[:span])
            put_lines(far, result[span:])

        if own_field is not None:
            own_p = rest.pop(0)

            @pl.when(here == 1)
            def _():
                run(moved, own_p)

        if own_residual is not None:
            own_r = rest.pop(0)

            @pl.when(here == 2)
            def _():
                run(own_r, moved)

    shape = jax.ShapeDtypeStruct((peers, rows, parts, planes, lanes), f32)
    return pl.pallas_call(
        kernel,
        grid=(rows,),
        in_specs=specs,
        out_specs=[rows_of(shape, 0)] * 2,
        out_shape=[shape] * 2,
        compiler_params=params(),
        cost_estimate=cost(6 * 4 * span * span * rows * nt, 20 * span * rows * nt),
        name="cross_terms",
    )(*operands)


def cells(layer, factors, moved, near, far, total, own_field, observed, next_field, old_residual, gradient, rows, held_back):
    own, own_t, beside = factors
    peers, _, parts, planes, _ = moved.shape
    span, nt = peers * planes, parts * lanes
    operands = [layer, *beside, moved, near, far, held_back]
    specs = [SMEM, whole((span, span)), whole((span, span)), rows_of(moved, 0), rows_of(near, 0), rows_of(far, 0), ANY]
    shape = jax.ShapeDtypeStruct((peers, rows, parts, planes, lanes), f32)
    shapes, out_specs, aliases = [], [], {}
    names = ["layer", "beside_high", "beside_low", "moved", "near", "far", "_"]
    out_names = []

    def take(name, array, spec):
        names.append(name)
        operands.append(array)
        specs.append(spec)

    def give(name, struct, spec):
        out_names.append(name)
        shapes.append(struct)
        out_specs.append(spec)

    if own_field is not None:
        take("own_high", own[0], whole((span, span)))
        take("own_low", own[1], whole((span, span)))
        take("field", own_field[0], rows_of(*own_field))
        table, first = observed
        band = 8 if table.shape[4] % 8 == 0 else table.shape[4]
        take("observed", table, pl.BlockSpec((peers, 2, parts, planes, band, lanes), lambda y: (0, 0, 0, 0, (first + y) // band, 0)))
        take("total", total, whole(total.shape))
        if next_field is not None:
            take("next_field", next_field[0], rows_of(*next_field))
            give("send", shape, rows_of(shape, 0))
        give("residual", shape, rows_of(shape, 0))
        give("new_total", jax.ShapeDtypeStruct(total.shape, f32), whole(total.shape))
    if old_residual is not None:
        take("own_t_high", own_t[0], whole((span, span)))
        take("own_t_low", own_t[1], whole((span, span)))
        take("old", old_residual, rows_of(old_residual, 0))
        buffer, high, start = gradient
        struct = jax.ShapeDtypeStruct((peers, high, parts, planes, lanes), f32)
        if buffer is not None:
            aliases[len(operands)] = len(shapes)
            take("buffer", buffer, ANY)
        give("gradient", struct, rows_of(struct, start))

    def kernel(*refs):
        ref = dict(zip(names + out_names, refs))
        here = ref["layer"][0]
        odd, upper = here % 2 == 1, here >= layers // 2
        extra = product((ref["beside_high"][...], ref["beside_low"][...]), split(lines(ref["moved"])))
        partial = jnp.where((here == 1) | (here == 2), lines(ref["near"]), lines(ref["far"]))
        if own_field is not None:
            log_rate = product((ref["own_high"][...], ref["own_low"][...]), split(lines(ref["field"])))
            log_rate += jnp.where(odd, extra, 0.0) + jnp.where(upper, partial, 0.0)
            row = lax.rem(first + pl.program_id(0), band)
            seen = ref["observed"]

            def pick(kind):
                one = lambda q, h: seen.at[q, kind, h].reshape(planes * band, lanes)[pl.ds(row, planes, stride=band), :]
                return jnp.concatenate([jnp.concatenate([one(q, h) for h in range(parts)], axis=1) for q in range(peers)], axis=0)

            observed_counts = pick(0)
            intensity = pick(1) * jnp.exp(log_rate)
            residual = observed_counts - intensity
            put_lines(ref["residual"], residual)

            @pl.when(pl.program_id(0) == 0)
            def _():
                ref["new_total"][...] = ref["total"][...]

            ref["new_total"][...] += fold_rows(observed_counts * log_rate - intensity)
            if next_field is not None:

                @pl.when(odd)
                def _():
                    put_lines(ref["send"], residual)

                @pl.when(jnp.logical_not(odd))
                def _():
                    ref["send"][...] = ref["next_field"][...]

        if old_residual is not None:
            out = product((ref["own_t_high"][...], ref["own_t_low"][...]), split(lines(ref["old"])))
            put_lines(ref["gradient"], out + jnp.where(odd, 0.0, extra) + jnp.where(upper, 0.0, partial))

    outs = pl.pallas_call(
        kernel,
        grid=(rows,),
        in_specs=specs,
        out_specs=out_specs,
        out_shape=shapes,
        input_output_aliases=aliases,
        compiler_params=params(),
        cost_estimate=cost(6 * 3 * span * span * rows * nt, 40 * span * rows * nt),
        name="cells",
    )(*operands)
    return dict(zip(out_names, outs))


def finish(groups, whitened, north, time):
    planes, ny, nt = whitened.shape
    step = 8
    flat = [g.reshape(-1, *g.shape[2:]) for g in groups]
    counts = [g.shape[0] for g in flat]
    parts = nt // lanes

    def kernel(w, north_high, north_low, time_high, time_low, *refs):
        out = refs[-1]
        north_pair = (north_high[...], north_low[...])
        time_pair = (time_high[...], time_low[...])

        def one(x, carry):
            line = lambda ref, rows, h: ref.reshape(rows * parts * step, lanes)[pl.ds(h * step + x, rows, stride=parts * step), :]
            values = jnp.concatenate(
                [jnp.concatenate([line(ref, rows, h) for h in range(parts)], axis=1) for ref, rows in zip(refs[:-1], counts)], axis=0
            )
            out[x] = product(north_pair, split(product(split(values), time_pair))) - w[x]
            return carry

        lax.fori_loop(0, step, one, 0, unroll=2)

    planes_block = pl.BlockSpec((step, ny, nt), lambda i: (i, 0, 0))
    return pl.pallas_call(
        kernel,
        grid=(planes // step,),
        in_specs=[planes_block] + [whole(f.shape) for f in (*north, *time)] + [pl.BlockSpec((rows, parts, step, lanes), lambda i: (0, 0, i, 0)) for rows in counts],
        out_specs=planes_block,
        out_shape=jax.ShapeDtypeStruct(whitened.shape, f32),
        compiler_params=params(),
        cost_estimate=cost(12 * planes * ny * nt * nt, 12 * whitened.size),
        name="finish",
    )(whitened, *north, *time, *flat)


def bounds_of(eighths, rows, unit):
    ends = sorted({min(rows, max(unit, rows * e // 8 // unit * unit)) for e in eighths} | {rows})
    return list(zip([0] + ends[:-1], ends))


def containing(bounds, row):
    return next(i for i, (low, high) in enumerate(bounds) if low <= row < high)


def per_device(whitened, counts, exposure, cholesky_east, cholesky_north, cholesky_time):
    devices = lax.axis_size("slab")
    peers = devices // layers
    planes, ny, nt = whitened.shape
    rows = ny // peers
    chunk = max(1, rows // chunk_target)
    number = rows // chunk
    unit = 8 if rows % 8 == 0 else rows
    layer = jnp.reshape(lax.axis_index("slab") // peers, (1,)).astype(jnp.int32)
    in_layer = [[z * peers + q for q in range(peers)] for z in range(layers)]

    def exchange(values):
        return lax.all_to_all(values, "slab", 0, 0, tiled=True, axis_index_groups=in_layer)

    def move(values, pairs):
        return lax.ppermute(values, "slab", [(a * peers + q, b * peers + q) for a, b in pairs for q in range(peers)])

    field_bounds = bounds_of((1, 4), rows, unit)
    cell_bounds = bounds_of((1, 2, 3, 4, 5, 6, 7), rows, unit)
    gradient_bounds = bounds_of((3, 5, 7), rows, chunk)

    tables = [packed(counts, exposure, *cell_bounds[0], peers, whitened)]
    tables[0] = exchange(tables[0])
    groups, squares = field(whitened, field_factors(cholesky_north, cholesky_time, field_bounds, peers), field_bounds, peers)
    fields = [exchange(g) for g in groups]
    north, time, cross, *blocks = other_factors(layer, cholesky_east, cholesky_north, cholesky_time, gradient_bounds, peers, squares)

    def field_chunk(c):
        g = containing(field_bounds, c * chunk)
        return fields[g], c * chunk - field_bounds[g][0]

    def field_slice(c):
        array, start = field_chunk(c)
        return lax.slice_in_dim(array, start, start + chunk, axis=1)

    total = -0.5 * squares
    crossed, residuals, nears, fars = {}, {}, {}, {}
    buffers, results = {}, {}

    def do_cross(k):
        own_field = field_chunk(k) if k < number else None
        own_residual = (residuals[k - 2], 0) if k >= 2 else None
        near, far = cross_terms(layer, cross, crossed[k], own_field, own_residual, chunk)
        forward, backward = k < number, k >= 2
        nears[k + 1] = move(near, [(1, 2)] * forward + [(2, 1)] * backward)
        fars[k + 1] = move(far, [(1, 3)] * forward + [(2, 0)] * backward)
        return near

    for k in (0, 1):
        crossed[k] = move(field_slice(k), [(0, 1), (2, 3)])
    done = do_cross(0)
    done = do_cross(1)
    for k in range(1, number + 3):
        c, g = k - 1, k - 3
        own_field = observed = next_field = old = gradient = None
        if c < number:
            own_field = field_chunk(c)
            t = containing(cell_bounds, c * chunk)
            while len(tables) <= t:
                held = residuals[c - 2 * unit // chunk] if c >= 2 * unit // chunk else done
                tables.append(exchange(packed(counts, exposure, *cell_bounds[len(tables)], peers, held)))
            observed = (tables[t], c * chunk - cell_bounds[t][0])
            if k + 1 < number:
                next_field = field_chunk(k + 1)
        if g >= 0:
            old = residuals[g]
            h = containing(gradient_bounds, g * chunk)
            low, high = gradient_bounds[h]
            gradient = (buffers.get(h), high - low, g * chunk - low)
        outs = cells(layer, blocks, crossed[k - 1], nears[k], fars[k], total, own_field, observed, next_field, old, gradient, chunk, done)
        if c < number:
            residuals[c], total = outs["residual"], outs["new_total"]
        if g >= 0:
            buffers[h] = outs["gradient"]
            if (g + 1) * chunk == high:
                results[h] = exchange(buffers[h])
        if k + 1 < number:
            crossed[k + 1] = move(outs["send"], [(0, 1), (2, 3), (1, 0), (3, 2)])
        elif k + 1 < number + 2:
            crossed[k + 1] = move(outs["residual"], [(1, 0), (3, 2)])
        if k + 1 in crossed:
            done = do_cross(k + 1)
    cell_count = planes * ny * nt * devices
    density = lax.psum(jnp.sum(total), "slab") / cell_count
    gradient = finish([results[h] for h in range(len(gradient_bounds))], whitened, north, time)
    return gradient, jnp.reshape(density, (1,))


def solution(mesh):
    placed = P(("chain", "slab"), None, None)
    return jax.shard_map(
        per_device,
        mesh=mesh,
        in_specs=(placed, placed, placed, P(), P(), P()),
        out_specs=(placed, P("chain")),
        check_vma=False,
    )
```

```python
import functools

import jax
import jax.numpy as jnp
from jax import lax
from jax.experimental import pallas as pl
from jax.experimental.pallas import tpu as pltpu
from jax.sharding import PartitionSpec as P

field_scale = 0.6
layers = 4
chunk_target = 16
lanes = 128
ends_of = {"field": (2, 6, 10), "cells": (2, 4, 6, 10, 14), "gradient": (7, 11, 14)}
transfers = (
    ("cells", 1, 1), ("cells", 2, 2), ("field", 2, 3), ("cells", 3, 4), ("field", 3, 6), ("cells", 4, 8), ("gradient", 0, 10),
    ("cells", 5, 12), ("gradient", 1, 13), ("gradient", 2, 16), ("gradient", 3, 18),
)
f32, bf16 = jnp.float32, jnp.bfloat16
ANY = pl.BlockSpec(memory_space=pl.ANY)
SMEM = pl.BlockSpec(memory_space=pltpu.SMEM)
params = functools.partial(pltpu.CompilerParams, vmem_limit_bytes=48 * 1024 * 1024)


def split(values):
    high = values.astype(bf16)
    return high, (values - high.astype(f32)).astype(bf16)


def dot(left, right):
    return jnp.dot(left, right, preferred_element_type=f32)


def product(left, right):
    return dot(left[0], right[0]) + (dot(left[0], right[1]) + dot(left[1], right[0]))


def whole(shape):
    return pl.BlockSpec(shape, lambda *_: (0,) * len(shape))


brief = pl.CostEstimate(flops=1, bytes_accessed=1, transcendentals=0)


def fold_rows(values):
    return jnp.sum(values.reshape(-1, 8, values.shape[-1]), axis=0)


def permuted_rows(matrix, bounds, peers):
    rows = matrix.shape[0] // peers
    return jnp.concatenate([matrix[q * rows + low : q * rows + high] for low, high in bounds for q in range(peers)], axis=0)


def field_factors(cholesky_north, cholesky_time, bounds, peers, held_back):
    def kernel(north, time, _, north_high, north_low, time_high, time_low):
        north_high[...], north_low[...] = split(permuted_rows(north[...], bounds, peers))
        time_high[...], time_low[...] = split(time[...].T)

    ny, nt = cholesky_north.shape[0], cholesky_time.shape[0]
    pair = lambda size: [jax.ShapeDtypeStruct((size, size), bf16)] * 2
    full = pl.BlockSpec(memory_space=pltpu.VMEM)
    return pl.pallas_call(
        kernel,
        out_shape=pair(ny) + pair(nt),
        in_specs=[full, full, ANY],
        out_specs=[full] * 4,
        cost_estimate=brief,
        compiler_params=params(),
        name="field_factors",
    )(cholesky_north, cholesky_time, held_back)


def other_factors(layer, cholesky_east, cholesky_north, cholesky_time, bounds, peers, held_back):
    nx = cholesky_east.shape[0]
    span, half = nx // layers, nx // 2

    def kernel(layer_ref, east, north, time, _, *outs):
        def put(place, values):
            outs[2 * place][...], outs[2 * place + 1][...] = split(values)

        here = layer_ref[0]
        put(0, permuted_rows(north[...], bounds, peers).T)
        put(1, time[...])

        @pl.when(here == 1)
        def _():
            put(2, field_scale * east[half:, :half])

        @pl.when(here != 1)
        def _():
            cross = (field_scale * east[half:, :half]).T
            put(2, jnp.concatenate([cross[span:], cross[:span]], axis=0))

        for z in range(layers):

            @pl.when(here == z)
            def _(z=z):
                own = field_scale * east[z * span : (z + 1) * span, z * span : (z + 1) * span]
                put(3, own)
                put(4, own.T)
                if z % 2:
                    put(5, field_scale * east[z * span : (z + 1) * span, (z - 1) * span : z * span])
                else:
                    put(5, (field_scale * east[(z + 1) * span : (z + 2) * span, z * span : (z + 1) * span]).T)

    ny, nt = cholesky_north.shape[0], cholesky_time.shape[0]
    sizes = (ny, nt, half, span, span, span)
    shapes = [jax.ShapeDtypeStruct((size, size), bf16) for size in sizes for _ in range(2)]
    outs = pl.pallas_call(
        kernel,
        out_shape=shapes,
        in_specs=[SMEM, whole((nx, nx)), whole((ny, ny)), whole((nt, nt)), ANY],
        out_specs=[whole(s.shape) for s in shapes],
        grid=(1,),
        compiler_params=params(),
        cost_estimate=brief,
        name="other_factors",
    )(layer, cholesky_east, cholesky_north, cholesky_time, held_back)
    return [tuple(outs[2 * i : 2 * i + 2]) for i in range(len(sizes))]


def field(whitened, factors, bounds, peers):
    planes, ny, nt = whitened.shape
    step = 8
    counts = [peers * (high - low) for low, high in bounds]
    parts = nt // lanes

    def kernel(w, north_high, north_low, time_high, time_low, *outs):
        squares = outs[-1]
        north = (north_high[...], north_low[...])
        time = (time_high[...], time_low[...])

        @pl.when(pl.program_id(0) == 0)
        def _():
            squares[...] = jnp.zeros_like(squares)

        def one(x, total):
            values = w[x]
            mixed = product(north, split(product(split(values), time)))
            start = 0
            for out, rows in zip(outs[:-1], counts):
                for h in range(parts):
                    out.reshape(rows * parts * step, lanes)[pl.ds(h * step + x, rows, stride=parts * step), :] = mixed[
                        start : start + rows, h * lanes : (h + 1) * lanes
                    ]
                start += rows
            return total + fold_rows(values * values)

        squares[...] += lax.fori_loop(0, step, one, jnp.zeros((8, nt), f32), unroll=2)

    *groups, squares = pl.pallas_call(
        kernel,
        grid=(planes // step,),
        in_specs=[pl.BlockSpec((step, ny, nt), lambda i: (i, 0, 0))] + [whole(f.shape) for f in factors],
        out_specs=[pl.BlockSpec((rows, parts, step, lanes), lambda i: (0, 0, i, 0)) for rows in counts] + [whole((8, nt))],
        out_shape=[jax.ShapeDtypeStruct((rows, parts, planes, lanes), f32) for rows in counts] + [jax.ShapeDtypeStruct((8, nt), f32)],
        compiler_params=params(),
        cost_estimate=brief,
        name="field",
    )(whitened, *factors)
    return [g.reshape(peers, -1, *g.shape[1:]) for g in groups], squares


def packed(counts, exposure, low, high, peers, *held_back):
    planes, ny, nt = counts.shape
    rows, parts = high - low, nt // lanes
    band = 8 if rows % 8 == 0 and low % 8 == 0 and (ny // peers) % 8 == 0 else rows
    per_peer = ny // peers // band

    def kernel(c, e, *rest):
        out = rest[-1]
        for h in range(parts):
            out[0, 0, h] = c[:, :, h * lanes : (h + 1) * lanes].astype(f32)
            out[0, 1, h] = e[:, :, h * lanes : (h + 1) * lanes].astype(f32)

    source = pl.BlockSpec((planes, band, nt), lambda q, j: (0, q * per_peer + low // band + j, 0))
    return pl.pallas_call(
        kernel,
        grid=(peers, rows // band),
        in_specs=[source, source] + [ANY] * len(held_back),
        out_specs=pl.BlockSpec((1, 2, parts, planes, band, lanes), lambda q, j: (q, 0, 0, 0, j, 0)),
        out_shape=jax.ShapeDtypeStruct((peers, 2, parts, planes, rows, lanes), f32),
        compiler_params=params(),
        cost_estimate=brief,
        name="packed",
    )(counts, exposure, *held_back)


def gate(values, *held_back):
    def kernel(*_):
        pass

    return pl.pallas_call(
        kernel,
        in_specs=[ANY] * (1 + len(held_back)),
        out_specs=ANY,
        out_shape=jax.ShapeDtypeStruct(values.shape, values.dtype),
        input_output_aliases={0: 0},
        cost_estimate=brief,
        name="gate",
    )(values, *held_back)


def lines(*blocks):
    peers = blocks[0].shape[0]
    return jnp.concatenate(
        [jnp.concatenate([b[q, 0, h] for b in blocks for h in range(b.shape[2])], axis=1) for q in range(peers)], axis=0
    )


def put_lines(outs, values):
    outs = outs if isinstance(outs, list) else [outs]
    first = 0
    for out in outs:
        peers, _, parts, planes, width = out.shape
        for q in range(peers):
            for h in range(parts):
                out[q, 0, h] = values[q * planes : (q + 1) * planes, (first + h) * width : (first + h + 1) * width]
        first += parts


def rows_of(array, start):
    peers, _, *rest = array.shape
    return pl.BlockSpec((peers, 1, *rest), lambda y: (0, start + y, 0, 0, 0))


def cross_terms(layer, cross, crossed, own_field, own_residual, rows):
    operands = [layer, *cross, *crossed]
    specs = [SMEM, whole(cross[0].shape), whole(cross[1].shape)] + [rows_of(c, 0) for c in crossed]
    pieces = len(crossed)
    for pair in (own_field, own_residual):
        if pair is not None:
            operands.append(pair[0])
            specs.append(rows_of(*pair))
    peers, _, _, planes, _ = crossed[0].shape
    parts = sum(c.shape[2] for c in crossed)
    span, nt = peers * planes, parts * lanes

    def kernel(layer_ref, high, low, *rest):
        moved, near, far = list(rest[:pieces]), *rest[-2:]
        rest = list(rest[pieces:-2])
        here = layer_ref[0]

        def run(first, second):
            result = product((high[...], low[...]), split(jnp.concatenate([lines(*first), lines(*second)], axis=0)))
            put_lines(near, result[:span])
            put_lines(far, result[span:])

        if own_field is not None:
            own_p = rest.pop(0)

            @pl.when(here == 1)
            def _():
                run(moved, [own_p])

        if own_residual is not None:
            own_r = rest.pop(0)

            @pl.when(here == 2)
            def _():
                run([own_r], moved)

    shape = jax.ShapeDtypeStruct((peers, rows, parts, planes, lanes), f32)
    return pl.pallas_call(
        kernel,
        grid=(rows,),
        in_specs=specs,
        out_specs=[rows_of(shape, 0)] * 2,
        out_shape=[shape] * 2,
        compiler_params=params(),
        cost_estimate=brief,
        name="cross_terms",
    )(*operands)


def cells(layer, factors, moved, near, far, total, own_field, observed, next_field, old_residual, gradient, rows, held_back):
    own, own_t, beside = factors
    peers, _, parts, planes, _ = near.shape
    span, nt = peers * planes, parts * lanes
    pieces = len(moved)
    operands = [layer, *beside, near, far, *moved, *held_back]
    specs = [SMEM, whole((span, span)), whole((span, span)), rows_of(near, 0), rows_of(far, 0)]
    specs += [rows_of(m, 0) for m in moved] + [ANY] * len(held_back)
    shape = jax.ShapeDtypeStruct((peers, rows, parts, planes, lanes), f32)
    shapes, out_specs, aliases = [], [], {}
    names = ["layer", "beside_high", "beside_low", "near", "far"]
    names += ["moved%d" % i for i in range(pieces)] + ["_"] * len(held_back)
    out_names = []

    def take(name, array, spec):
        names.append(name)
        operands.append(array)
        specs.append(spec)

    def give(name, struct, spec):
        out_names.append(name)
        shapes.append(struct)
        out_specs.append(spec)

    if own_field is not None:
        take("own_high", own[0], whole((span, span)))
        take("own_low", own[1], whole((span, span)))
        take("field", own_field[0], rows_of(*own_field))
        table, first = observed
        band = 8 if table.shape[4] % 8 == 0 else table.shape[4]
        take("observed", table, pl.BlockSpec((peers, 2, parts, planes, band, lanes), lambda y: (0, 0, 0, 0, (first + y) // band, 0)))
        take("total", total, whole(total.shape))
        if next_field is not None:
            take("next_field", next_field[0], rows_of(*next_field))
        for i in range(pieces):
            piece = jax.ShapeDtypeStruct((peers, rows, moved[i].shape[2], planes, lanes), f32)
            give("send%d" % i, piece, rows_of(piece, 0))
        give("residual", shape, rows_of(shape, 0))
        give("new_total", jax.ShapeDtypeStruct(total.shape, f32), whole(total.shape))
    if old_residual is not None:
        take("own_t_high", own_t[0], whole((span, span)))
        take("own_t_low", own_t[1], whole((span, span)))
        take("old", old_residual, rows_of(old_residual, 0))
        buffer, high, start = gradient
        struct = jax.ShapeDtypeStruct((peers, high, parts, planes, lanes), f32)
        if buffer is not None:
            aliases[len(operands)] = len(shapes)
            take("buffer", buffer, ANY)
        give("gradient", struct, rows_of(struct, start))

    def kernel(*refs):
        ref = dict(zip(names + out_names, refs))
        here = ref["layer"][0]
        odd, upper = here % 2 == 1, here >= layers // 2
        extra = product((ref["beside_high"][...], ref["beside_low"][...]), split(lines(*[ref["moved%d" % i] for i in range(pieces)])))
        partial = jnp.where((here == 1) | (here == 2), lines(ref["near"]), lines(ref["far"]))
        if own_field is not None:
            log_rate = product((ref["own_high"][...], ref["own_low"][...]), split(lines(ref["field"])))
            log_rate += jnp.where(odd, extra, 0.0) + jnp.where(upper, partial, 0.0)
            row = lax.rem(first + pl.program_id(0), band)
            seen = ref["observed"]

            def pick(kind):
                one = lambda q, h: seen.at[q, kind, h].reshape(planes * band, lanes)[pl.ds(row, planes, stride=band), :]
                return jnp.concatenate([jnp.concatenate([one(q, h) for h in range(parts)], axis=1) for q in range(peers)], axis=0)

            observed_counts = pick(0)
            intensity = pick(1) * jnp.exp(log_rate)
            residual = observed_counts - intensity
            put_lines(ref["residual"], residual)

            @pl.when(pl.program_id(0) == 0)
            def _():
                ref["new_total"][...] = ref["total"][...]

            ref["new_total"][...] += fold_rows(observed_counts * log_rate - intensity)
            send = [ref["send%d" % i] for i in range(pieces)]

            @pl.when(odd)
            def _():
                put_lines(send, residual)

            if next_field is not None:

                @pl.when(jnp.logical_not(odd))
                def _():
                    put_lines(send, lines(ref["next_field"]))

        if old_residual is not None:
            out = product((ref["own_t_high"][...], ref["own_t_low"][...]), split(lines(ref["old"])))
            put_lines(ref["gradient"], out + jnp.where(odd, 0.0, extra) + jnp.where(upper, 0.0, partial))

    outs = pl.pallas_call(
        kernel,
        grid=(rows,),
        in_specs=specs,
        out_specs=out_specs,
        out_shape=shapes,
        input_output_aliases=aliases,
        compiler_params=params(),
        cost_estimate=brief,
        name="cells",
    )(*operands)
    return dict(zip(out_names, outs))


def finish(groups, whitened, north, time):
    planes, ny, nt = whitened.shape
    step = 8
    flat = [g.reshape(-1, *g.shape[2:]) for g in groups]
    counts = [g.shape[0] for g in flat]
    parts = nt // lanes

    def kernel(w, north_high, north_low, time_high, time_low, *refs):
        out = refs[-1]
        north_pair = (north_high[...], north_low[...])
        time_pair = (time_high[...], time_low[...])

        def one(x, carry):
            line = lambda ref, rows, h: ref.reshape(rows * parts * step, lanes)[pl.ds(h * step + x, rows, stride=parts * step), :]
            values = jnp.concatenate(
                [jnp.concatenate([line(ref, rows, h) for h in range(parts)], axis=1) for ref, rows in zip(refs[:-1], counts)], axis=0
            )
            out[x] = product(north_pair, split(product(split(values), time_pair))) - w[x]
            return carry

        lax.fori_loop(0, step, one, 0, unroll=2)

    planes_block = pl.BlockSpec((step, ny, nt), lambda i: (i, 0, 0))
    return pl.pallas_call(
        kernel,
        grid=(planes // step,),
        in_specs=[planes_block] + [whole(f.shape) for f in (*north, *time)] + [pl.BlockSpec((rows, parts, step, lanes), lambda i: (0, 0, i, 0)) for rows in counts],
        out_specs=planes_block,
        out_shape=jax.ShapeDtypeStruct(whitened.shape, f32),
        compiler_params=params(),
        cost_estimate=brief,
        name="finish",
    )(whitened, *north, *time, *flat)


def ranges_of(kind, rows, unit):
    unit = unit if kind == "cells" else max(1, rows // chunk_target)
    ends = sorted({min(rows, max(unit, rows * e // 16 // unit * unit)) for e in ends_of[kind]} | {rows})
    return list(zip([0] + ends[:-1], ends))


def per_device(whitened, counts, exposure, cholesky_east, cholesky_north, cholesky_time):
    devices = lax.axis_size("slab")
    peers = devices // layers
    planes, ny, nt = whitened.shape
    rows = ny // peers
    chunk = max(1, rows // chunk_target)
    number = rows // chunk
    unit = 8 if rows % 8 == 0 else rows
    layer = jnp.reshape(lax.axis_index("slab") // peers, (1,)).astype(jnp.int32)
    in_layer = [[z * peers + q for q in range(peers)] for z in range(layers)]

    def exchange(values):
        return lax.all_to_all(values, "slab", 0, 0, tiled=True, axis_index_groups=in_layer)

    def move(values, pairs):
        return lax.ppermute(values, "slab", [(a * peers + q, b * peers + q) for a, b in pairs for q in range(peers)])

    spans = {kind: ranges_of(kind, rows, unit) for kind in ("field", "cells", "gradient")}
    pack = lambda i, *held_back: packed(counts, exposure, *spans["cells"][i], peers, *held_back)
    first = pack(0)
    arrived = {("cells", 0): exchange(first)}
    factors = field_factors(cholesky_north, cholesky_time, spans["field"], peers, first)
    groups, squares = field(whitened, factors, spans["field"], peers)
    start = gate(groups[0], arrived["cells", 0])
    tables = [first] + [pack(i, start) for i in range(1, len(spans["cells"]))]
    north, time, cross, *blocks = other_factors(layer, cholesky_east, cholesky_north, cholesky_time, spans["gradient"], peers, start)
    arrived["field", 0] = gate(exchange(start), *tables[1:], cross[0])

    def sum_over_slab(values):
        if devices & (devices - 1):
            return lax.psum(values, "slab")
        step = 1
        while step < devices:
            values = values + lax.ppermute(values, "slab", [(q, q ^ step) for q in range(devices)])
            step *= 2
        return values

    def part_of(kind, c):
        i = next(i for i, (low, high) in enumerate(spans[kind]) if low <= c * chunk < high)
        return i, c * chunk - spans[kind][i][0]

    def field_chunk(c):
        i, start = part_of("field", c)
        return arrived["field", i], start

    def pieces_of(values):
        half = max(1, nt // lanes // 2)
        return [lax.slice_in_dim(values, h, min(h + half, nt // lanes), axis=2) for h in range(0, nt // lanes, half)]

    total = -0.5 * squares
    crossed, residuals, nears, fars = {}, {}, {}, {}
    buffers = {}

    def do_cross(k):
        own_field = field_chunk(k) if k < number else None
        own_residual = (residuals[k - 2], 0) if k >= 2 else None
        near, far = cross_terms(layer, cross, crossed[k], own_field, own_residual, chunk)
        forward, backward = k < number, k >= 2
        nears[k + 1] = move(near, [(1, 2)] * forward + [(2, 1)] * backward)
        fars[k + 1] = move(far, [(1, 3)] * forward + [(2, 0)] * backward)
        return near

    def send(kind, i, held_back):
        values = {"field": groups, "cells": tables, "gradient": buffers}[kind][i]
        arrived[kind, i] = exchange(gate(values, held_back) if held_back is not None else values)

    for k in (0, 1):
        array, start = field_chunk(k)
        values = lax.slice_in_dim(array, start, start + chunk, axis=1)
        crossed[k] = [move(v, [(0, 1), (2, 3)]) for v in pieces_of(values)]
        if k == 0:
            send("field", 1, values)
            done = do_cross(0)
    done = do_cross(1)
    pending = list(transfers)
    for k in range(1, number + 3):
        c, g = k - 1, k - 3
        held = [done] if k < number + 2 else [done, sums]
        own_field = observed = next_field = old = gradient = None
        early = residuals[min(k - 2, number - 1)] if k >= 2 else done
        while pending and pending[0][2] * number <= (k - 1) * 16:
            kind, i, _ = pending.pop(0)
            if i < len(spans[kind]):
                send(kind, i, early)
        if c < number:
            own_field = field_chunk(c)
            i, start = part_of("cells", c)
            observed = (arrived["cells", i], start)
            if k + 1 < number:
                next_field = field_chunk(k + 1)
        if g >= 0:
            old = residuals[g]
            h, start = part_of("gradient", g)
            low, high = spans["gradient"][h]
            gradient = (buffers.get(h), high - low, start)
        outs = cells(layer, blocks, crossed[k - 1], nears[k], fars[k], total, own_field, observed, next_field, old, gradient, chunk, held)
        if c < number:
            residuals[c], total = outs["residual"], outs["new_total"]
            if c == number - 1:
                sums = sum_over_slab(total)
        if g >= 0:
            buffers[h] = outs["gradient"]
        if c < number:
            pairs = ([(0, 1), (2, 3)] if k + 1 < number else []) + [(1, 0), (3, 2)]
            crossed[k + 1] = [move(outs["send%d" % i], pairs) for i in range(len(crossed[0]))]
            done = do_cross(k + 1)
    for kind, i, _ in pending:
        if i < len(spans[kind]):
            send(kind, i, None)
    cell_count = planes * ny * nt * devices
    density = jnp.sum(sums) / cell_count
    gradient = finish([arrived["gradient", h] for h in range(len(spans["gradient"]))], whitened, north, time)
    return gradient, jnp.reshape(density, (1,))


def solution(mesh):
    placed = P(("chain", "slab"), None, None)
    return jax.shard_map(
        per_device,
        mesh=mesh,
        in_specs=(placed, placed, placed, P(), P(), P()),
        out_specs=(placed, P("chain")),
        check_vma=False,
    )
```

```python
import functools

import jax
import jax.numpy as jnp
from jax import lax
from jax.experimental import pallas as pl
from jax.experimental.pallas import tpu as pltpu
from jax.sharding import PartitionSpec as P

field_scale = 0.6
layers = 4
chunk_target = 16
lanes = 128
ends_of = {"field": (2, 10), "cells": (2, 6, 10), "gradient": (7, 11, 14)}
transfers = (
    ("cells", 1, 1), ("cells", 2, 3), ("field", 2, 5), ("cells", 3, 7), ("gradient", 0, 11), ("gradient", 1, 14), ("gradient", 2, 17), ("gradient", 3, 19),
)
f32, bf16 = jnp.float32, jnp.bfloat16
ANY = pl.BlockSpec(memory_space=pl.ANY)
SMEM = pl.BlockSpec(memory_space=pltpu.SMEM)
params = functools.partial(pltpu.CompilerParams, vmem_limit_bytes=48 * 1024 * 1024)


def split(values):
    high = values.astype(bf16)
    return high, (values - high.astype(f32)).astype(bf16)


def dot(left, right):
    return jnp.dot(left, right, preferred_element_type=f32)


def product(left, right):
    return dot(left[0], right[0]) + (dot(left[0], right[1]) + dot(left[1], right[0]))


def whole(shape):
    return pl.BlockSpec(shape, lambda *_: (0,) * len(shape))


brief = pl.CostEstimate(flops=1, bytes_accessed=1, transcendentals=0)
step_long = pl.CostEstimate(flops=1, bytes_accessed=60_000_000, transcendentals=0)


def fold_rows(values):
    return jnp.sum(values.reshape(-1, 8, values.shape[-1]), axis=0)


def permuted_rows(matrix, bounds, peers):
    rows = matrix.shape[0] // peers
    return jnp.concatenate([matrix[q * rows + low : q * rows + high] for low, high in bounds for q in range(peers)], axis=0)


def field_factors(cholesky_north, cholesky_time, bounds, peers, held_back):
    def kernel(north, time, _, north_high, north_low, time_high, time_low):
        north_high[...], north_low[...] = split(permuted_rows(north[...], bounds, peers))
        time_high[...], time_low[...] = split(time[...].T)

    ny, nt = cholesky_north.shape[0], cholesky_time.shape[0]
    pair = lambda size: [jax.ShapeDtypeStruct((size, size), bf16)] * 2
    full = pl.BlockSpec(memory_space=pltpu.VMEM)
    return pl.pallas_call(
        kernel,
        out_shape=pair(ny) + pair(nt),
        in_specs=[full, full, ANY],
        out_specs=[full] * 4,
        cost_estimate=brief,
        compiler_params=params(),
        name="field_factors",
    )(cholesky_north, cholesky_time, held_back)


def other_factors(layer, cholesky_east, cholesky_north, cholesky_time, bounds, peers, held_back):
    nx = cholesky_east.shape[0]
    span, half = nx // layers, nx // 2
    most = bounds[-1][0] * peers

    def kernel(layer_ref, east, north, time, _, *outs):
        def put(place, values):
            outs[2 * place][...], outs[2 * place + 1][...] = split(values)

        here = layer_ref[0]
        turned = permuted_rows(north[...], bounds, peers).T
        put(0, turned[:, :most])
        put(1, turned[:, most:])
        put(2, time[...])

        @pl.when(here == 1)
        def _():
            put(3, field_scale * east[half:, :half])

        @pl.when(here != 1)
        def _():
            cross = (field_scale * east[half:, :half]).T
            put(3, jnp.concatenate([cross[span:], cross[:span]], axis=0))

        for z in range(layers):

            @pl.when(here == z)
            def _(z=z):
                own = field_scale * east[z * span : (z + 1) * span, z * span : (z + 1) * span]
                put(4, own)
                put(5, own.T)
                if z % 2:
                    put(6, field_scale * east[z * span : (z + 1) * span, (z - 1) * span : z * span])
                else:
                    put(6, (field_scale * east[(z + 1) * span : (z + 2) * span, z * span : (z + 1) * span]).T)

    ny, nt = cholesky_north.shape[0], cholesky_time.shape[0]
    sizes = [(ny, most), (ny, ny - most)] + [(size, size) for size in (nt, half, span, span, span)]
    shapes = [jax.ShapeDtypeStruct(size, bf16) for size in sizes for _ in range(2)]
    outs = pl.pallas_call(
        kernel,
        out_shape=shapes,
        in_specs=[SMEM, whole((nx, nx)), whole((ny, ny)), whole((nt, nt)), ANY],
        out_specs=[whole(s.shape) for s in shapes],
        grid=(1,),
        compiler_params=params(),
        cost_estimate=brief,
        name="other_factors",
    )(layer, cholesky_east, cholesky_north, cholesky_time, held_back)
    return [tuple(outs[2 * i : 2 * i + 2]) for i in range(len(sizes))]


def field(whitened, factors, bounds, peers):
    planes, ny, nt = whitened.shape
    step = 8
    counts = [peers * (high - low) for low, high in bounds]
    parts = nt // lanes

    def kernel(w, north_high, north_low, time_high, time_low, *outs):
        squares = outs[-1]
        north = (north_high[...], north_low[...])
        time = (time_high[...], time_low[...])

        @pl.when(pl.program_id(0) == 0)
        def _():
            squares[...] = jnp.zeros_like(squares)

        def one(x, total):
            values = w[x]
            mixed = product(north, split(product(split(values), time)))
            start = 0
            for out, rows in zip(outs[:-1], counts):
                for h in range(parts):
                    out.reshape(rows * parts * step, lanes)[pl.ds(h * step + x, rows, stride=parts * step), :] = mixed[
                        start : start + rows, h * lanes : (h + 1) * lanes
                    ]
                start += rows
            return total + fold_rows(values * values)

        squares[...] += lax.fori_loop(0, step, one, jnp.zeros((8, nt), f32), unroll=2)

    *groups, squares = pl.pallas_call(
        kernel,
        grid=(planes // step,),
        in_specs=[pl.BlockSpec((step, ny, nt), lambda i: (i, 0, 0))] + [whole(f.shape) for f in factors],
        out_specs=[pl.BlockSpec((rows, parts, step, lanes), lambda i: (0, 0, i, 0)) for rows in counts] + [whole((8, nt))],
        out_shape=[jax.ShapeDtypeStruct((rows, parts, planes, lanes), f32) for rows in counts] + [jax.ShapeDtypeStruct((8, nt), f32)],
        compiler_params=params(),
        cost_estimate=brief,
        name="field",
    )(whitened, *factors)
    return [g.reshape(peers, -1, *g.shape[1:]) for g in groups], squares


def packed(counts, exposure, low, high, peers, *held_back):
    planes, ny, nt = counts.shape
    rows, parts = high - low, nt // lanes
    band = 8 if rows % 8 == 0 and low % 8 == 0 and (ny // peers) % 8 == 0 else rows
    per_peer = ny // peers // band

    def kernel(c, e, *rest):
        out = rest[-1]
        for h in range(parts):
            out[0, 0, h] = c[:, :, h * lanes : (h + 1) * lanes].astype(f32)
            out[0, 1, h] = e[:, :, h * lanes : (h + 1) * lanes].astype(f32)

    source = pl.BlockSpec((planes, band, nt), lambda q, j: (0, q * per_peer + low // band + j, 0))
    return pl.pallas_call(
        kernel,
        grid=(peers, rows // band),
        in_specs=[source, source] + [ANY] * len(held_back),
        out_specs=pl.BlockSpec((1, 2, parts, planes, band, lanes), lambda q, j: (q, 0, 0, 0, j, 0)),
        out_shape=jax.ShapeDtypeStruct((peers, 2, parts, planes, rows, lanes), f32),
        compiler_params=params(),
        cost_estimate=brief,
        name="packed",
    )(counts, exposure, *held_back)


def gate(values, *held_back):
    def kernel(*_):
        pass

    return pl.pallas_call(
        kernel,
        in_specs=[ANY] * (1 + len(held_back)),
        out_specs=ANY,
        out_shape=jax.ShapeDtypeStruct(values.shape, values.dtype),
        input_output_aliases={0: 0},
        cost_estimate=brief,
        name="gate",
    )(values, *held_back)


def lines(*blocks):
    peers = blocks[0].shape[0]
    return jnp.concatenate(
        [jnp.concatenate([b[q, 0, h] for b in blocks for h in range(b.shape[2])], axis=1) for q in range(peers)], axis=0
    )


def put_lines(outs, values):
    outs = outs if isinstance(outs, list) else [outs]
    first = 0
    for out in outs:
        peers, _, parts, planes, width = out.shape
        for q in range(peers):
            for h in range(parts):
                out[q, 0, h] = values[q * planes : (q + 1) * planes, (first + h) * width : (first + h + 1) * width]
        first += parts


def rows_of(array, start):
    peers, _, *rest = array.shape
    return pl.BlockSpec((peers, 1, *rest), lambda y: (0, start + y, 0, 0, 0))


def cross_terms(layer, cross, crossed, own_field, own_residual, rows, *held_back):
    operands = [layer, *cross, *crossed]
    specs = [SMEM, whole(cross[0].shape), whole(cross[1].shape)] + [rows_of(c, 0) for c in crossed]
    pieces = len(crossed)
    for pair in (own_field, own_residual):
        if pair is not None:
            operands.append(pair[0])
            specs.append(rows_of(*pair))
    operands += held_back
    specs += [ANY] * len(held_back)
    peers, _, _, planes, _ = crossed[0].shape
    parts = sum(c.shape[2] for c in crossed)
    span, nt = peers * planes, parts * lanes

    def kernel(layer_ref, high, low, *rest):
        moved, near, far = list(rest[:pieces]), *rest[-2:]
        rest = list(rest[pieces:-2])
        here = layer_ref[0]

        def run(first, second):
            result = product((high[...], low[...]), split(jnp.concatenate([lines(*first), lines(*second)], axis=0)))
            put_lines(near, result[:span])
            put_lines(far, result[span:])

        if own_field is not None:
            own_p = rest.pop(0)

            @pl.when(here == 1)
            def _():
                run(moved, [own_p])

        if own_residual is not None:
            own_r = rest.pop(0)

            @pl.when(here == 2)
            def _():
                run([own_r], moved)

    shape = jax.ShapeDtypeStruct((peers, rows, parts, planes, lanes), f32)
    return pl.pallas_call(
        kernel,
        grid=(rows,),
        in_specs=specs,
        out_specs=[rows_of(shape, 0)] * 2,
        out_shape=[shape] * 2,
        compiler_params=params(),
        cost_estimate=brief,
        name="cross_terms",
    )(*operands)


def cells(layer, factors, moved, near, far, total, own_field, observed, next_field, old_residual, gradient, rows, held_back):
    own, own_t, beside = factors
    peers, _, parts, planes, _ = near.shape
    span, nt = peers * planes, parts * lanes
    pieces = len(moved)
    operands = [layer, *beside, near, far, *moved, *held_back]
    specs = [SMEM, whole((span, span)), whole((span, span)), rows_of(near, 0), rows_of(far, 0)]
    specs += [rows_of(m, 0) for m in moved] + [ANY] * len(held_back)
    shape = jax.ShapeDtypeStruct((peers, rows, parts, planes, lanes), f32)
    shapes, out_specs, aliases = [], [], {}
    names = ["layer", "beside_high", "beside_low", "near", "far"]
    names += ["moved%d" % i for i in range(pieces)] + ["_"] * len(held_back)
    out_names = []

    def take(name, array, spec):
        names.append(name)
        operands.append(array)
        specs.append(spec)

    def give(name, struct, spec):
        out_names.append(name)
        shapes.append(struct)
        out_specs.append(spec)

    if own_field is not None:
        take("own_high", own[0], whole((span, span)))
        take("own_low", own[1], whole((span, span)))
        take("field", own_field[0], rows_of(*own_field))
        table, first = observed
        band = 8 if table.shape[4] % 8 == 0 else table.shape[4]
        take("observed", table, pl.BlockSpec((peers, 2, parts, planes, band, lanes), lambda y: (0, 0, 0, 0, (first + y) // band, 0)))
        take("total", total, whole(total.shape))
        if next_field is not None:
            take("next_field", next_field[0], rows_of(*next_field))
        for i in range(pieces):
            piece = jax.ShapeDtypeStruct((peers, rows, moved[i].shape[2], planes, lanes), f32)
            give("send%d" % i, piece, rows_of(piece, 0))
        give("residual", shape, rows_of(shape, 0))
        give("new_total", jax.ShapeDtypeStruct(total.shape, f32), whole(total.shape))
    if old_residual is not None:
        take("own_t_high", own_t[0], whole((span, span)))
        take("own_t_low", own_t[1], whole((span, span)))
        take("old", old_residual, rows_of(old_residual, 0))
        buffer, high, start = gradient
        struct = jax.ShapeDtypeStruct((peers, high, parts, planes, lanes), f32)
        if buffer is not None:
            aliases[len(operands)] = len(shapes)
            take("buffer", buffer, ANY)
        give("gradient", struct, rows_of(struct, start))

    def kernel(*refs):
        ref = dict(zip(names + out_names, refs))
        here = ref["layer"][0]
        odd, upper = here % 2 == 1, here >= layers // 2
        extra = product((ref["beside_high"][...], ref["beside_low"][...]), split(lines(*[ref["moved%d" % i] for i in range(pieces)])))
        partial = jnp.where((here == 1) | (here == 2), lines(ref["near"]), lines(ref["far"]))
        if own_field is not None:
            log_rate = product((ref["own_high"][...], ref["own_low"][...]), split(lines(ref["field"])))
            log_rate += jnp.where(odd, extra, 0.0) + jnp.where(upper, partial, 0.0)
            row = lax.rem(first + pl.program_id(0), band)
            seen = ref["observed"]

            def pick(kind):
                one = lambda q, h: seen.at[q, kind, h].reshape(planes * band, lanes)[pl.ds(row, planes, stride=band), :]
                return jnp.concatenate([jnp.concatenate([one(q, h) for h in range(parts)], axis=1) for q in range(peers)], axis=0)

            observed_counts = pick(0)
            intensity = pick(1) * jnp.exp(log_rate)
            residual = observed_counts - intensity
            put_lines(ref["residual"], residual)

            @pl.when(pl.program_id(0) == 0)
            def _():
                ref["new_total"][...] = ref["total"][...]

            ref["new_total"][...] += fold_rows(observed_counts * log_rate - intensity)
            send = [ref["send%d" % i] for i in range(pieces)]

            @pl.when(odd)
            def _():
                put_lines(send, residual)

            if next_field is not None:

                @pl.when(jnp.logical_not(odd))
                def _():
                    put_lines(send, lines(ref["next_field"]))

        if old_residual is not None:
            out = product((ref["own_t_high"][...], ref["own_t_low"][...]), split(lines(ref["old"])))
            put_lines(ref["gradient"], out + jnp.where(odd, 0.0, extra) + jnp.where(upper, 0.0, partial))

    outs = pl.pallas_call(
        kernel,
        grid=(rows,),
        in_specs=specs,
        out_specs=out_specs,
        out_shape=shapes,
        input_output_aliases=aliases,
        compiler_params=params(),
        cost_estimate=step_long,
        name="cells",
    )(*operands)
    return dict(zip(out_names, outs))


def finish(groups, partial, north, time, sign):
    planes, ny, nt = partial.shape
    step = 8
    flat = [g.reshape(-1, *g.shape[2:]) for g in groups]
    counts = [g.shape[0] for g in flat]
    parts = nt // lanes

    def kernel(w, north_high, north_low, time_high, time_low, *refs):
        out = refs[-1]
        north_pair = (north_high[...], north_low[...])
        time_pair = (time_high[...], time_low[...])

        def one(x, carry):
            line = lambda ref, rows, h: ref.reshape(rows * parts * step, lanes)[pl.ds(h * step + x, rows, stride=parts * step), :]
            values = jnp.concatenate(
                [jnp.concatenate([line(ref, rows, h) for h in range(parts)], axis=1) for ref, rows in zip(refs[:-1], counts)], axis=0
            )
            out[x] = product(north_pair, split(product(split(values), time_pair))) + sign * w[x]
            return carry

        lax.fori_loop(0, step, one, 0, unroll=2)

    planes_block = pl.BlockSpec((step, ny, nt), lambda i: (i, 0, 0))
    return pl.pallas_call(
        kernel,
        grid=(planes // step,),
        in_specs=[planes_block]
        + [whole(f.shape) for f in (*north, *time)]
        + [pl.BlockSpec((rows, parts, step, lanes), lambda i: (0, 0, i, 0)) for rows in counts],
        out_specs=planes_block,
        out_shape=jax.ShapeDtypeStruct(partial.shape, f32),
        compiler_params=params(),
        cost_estimate=brief,
        name="finish",
    )(partial, *north, *time, *flat)


def ranges_of(kind, rows, unit):
    unit = unit if kind == "cells" else max(1, rows // chunk_target)
    ends = sorted({min(rows, max(unit, rows * e // 16 // unit * unit)) for e in ends_of[kind]} | {rows})
    return list(zip([0] + ends[:-1], ends))


def per_device(whitened, counts, exposure, cholesky_east, cholesky_north, cholesky_time):
    devices = lax.axis_size("slab")
    peers = devices // layers
    planes, ny, nt = whitened.shape
    rows = ny // peers
    chunk = max(1, rows // chunk_target)
    number = rows // chunk
    unit = 8 if rows % 8 == 0 else rows
    layer = jnp.reshape(lax.axis_index("slab") // peers, (1,)).astype(jnp.int32)
    in_layer = [[z * peers + q for q in range(peers)] for z in range(layers)]

    def exchange(values):
        return lax.all_to_all(values, "slab", 0, 0, tiled=True, axis_index_groups=in_layer)

    def move(values, pairs):
        return lax.ppermute(values, "slab", [(a * peers + q, b * peers + q) for a, b in pairs for q in range(peers)])

    spans = {kind: ranges_of(kind, rows, unit) for kind in ("field", "cells", "gradient")}
    pack = lambda i, *held_back: packed(counts, exposure, *spans["cells"][i], peers, *held_back)
    first = pack(0)
    arrived = {("cells", 0): exchange(first)}
    factors = field_factors(cholesky_north, cholesky_time, spans["field"], peers, first)
    groups, squares = field(whitened, factors, spans["field"], peers)
    start = gate(groups[0], arrived["cells", 0])
    tables = [first, pack(1, start)]
    north, north_last, time, cross, *blocks = other_factors(layer, cholesky_east, cholesky_north, cholesky_time, spans["gradient"], peers, start)
    arrived["field", 0] = gate(exchange(start), *tables[1:], cross[0])

    def sums_over_slab(values):
        if devices & (devices - 1):
            yield lax.psum(values, "slab")
        step = 1
        while step < devices and not devices & (devices - 1):
            values = values + lax.ppermute(values, "slab", [(q, q ^ step) for q in range(devices)])
            yield values
            step *= 2

    def part_of(kind, c):
        i = next(i for i, (low, high) in enumerate(spans[kind]) if low <= c * chunk < high)
        return i, c * chunk - spans[kind][i][0]

    def field_chunk(c):
        i, start = part_of("field", c)
        return arrived["field", i], start

    total = -0.5 * squares
    crossed, residuals, nears, fars = {}, {}, {}, {}
    buffers = {}
    latest = [arrived["field", 0]]

    def do_cross(k, *held_back):
        own_field = field_chunk(k) if k < number else None
        own_residual = (residuals[k - 3], 0) if k >= 3 else None
        near, far = cross_terms(layer, cross, crossed[k - 1], own_field, own_residual, chunk, *held_back)
        forward, backward = k < number, k >= 3
        nears[k + 1] = move(near, [(1, 2)] * forward + [(2, 1)] * backward)
        fars[k + 1] = move(far, [(1, 3)] * forward + [(2, 0)] * backward)
        return near

    def send(kind, i, held_back):
        values = {"field": groups, "cells": tables, "gradient": buffers}[kind][i]
        latest[0] = arrived[kind, i] = exchange(gate(values, *latest, *([] if held_back is None else [held_back])))

    def start_field(k):
        array, start = field_chunk(k + 1)
        values = lax.slice_in_dim(array, start, start + chunk, axis=1)
        crossed[k] = [move(values, [(0, 1), (2, 3)])]
        return values

    start_field(-1)
    send("field", 1, start_field(0))
    near = do_cross(0)
    tables += [pack(i, near) for i in range(2, len(spans["cells"]))]
    start_field(1)
    done = do_cross(1, nears[1], *tables[2:])
    pending = list(transfers)
    for k in range(1, number + 4):
        c, g = k - 1, k - 4
        own_field = observed = next_field = old = gradient = None
        while pending and pending[0][2] * number <= (k - 1) * 16:
            kind, i, _ = pending.pop(0)
            if i < len(spans[kind]):
                send(kind, i, residuals[min(k - 2, number - 1)] if k >= 2 else done)
        if c < number:
            own_field = field_chunk(c)
            i, start = part_of("cells", c)
            observed = (arrived["cells", i], start)
            if k + 2 < number:
                next_field = field_chunk(k + 2)
        if g >= 0:
            old = residuals[g]
            h, start = part_of("gradient", g)
            low, high = spans["gradient"][h]
            gradient = (buffers.get(h), high - low, start)
        held = [done] if k < number + 3 else []
        if k == number + 1:
            sum_steps = sums_over_slab(total)
        if k > number:
            held.append(next(sum_steps))
        outs = cells(layer, blocks, crossed[k - 2], nears[k], fars[k], total, own_field, observed, next_field, old, gradient, chunk, held)
        if c < number:
            residuals[c], total = outs["residual"], outs["new_total"]
        if g >= 0:
            buffers[h] = outs["gradient"]
        if c < number:
            pairs = ([(0, 1), (2, 3)] if k + 2 < number else []) + [(1, 0), (3, 2)]
            crossed[k + 1] = [move(outs["send%d" % i], pairs) for i in range(len(crossed[0]))]
        if k + 1 <= number + 2:
            done = do_cross(k + 1)
    for kind, i, _ in pending:
        if i < len(spans[kind]):
            send(kind, i, None)
    for sums in sum_steps:
        pass
    cell_count = planes * ny * nt * devices
    density = jnp.sum(sums) / cell_count
    *most, last = [arrived["gradient", h] for h in range(len(spans["gradient"]))]
    gradient = finish(most, whitened, north, time, -1.0) if most else whitened
    gradient = finish([last], gradient, north_last, time, 1.0 if most else -1.0)
    return gradient, jnp.reshape(density, (1,))


def solution(mesh):
    placed = P(("chain", "slab"), None, None)
    return jax.shard_map(
        per_device,
        mesh=mesh,
        in_specs=(placed, placed, placed, P(), P(), P()),
        out_specs=(placed, P("chain")),
        check_vma=False,
    )
```

```python
import functools

import jax
import jax.numpy as jnp
from jax import lax
from jax.experimental import pallas as pl
from jax.experimental.pallas import tpu as pltpu
from jax.sharding import PartitionSpec as P

field_scale = 0.6
layers = 4
chunk_target = 16
lanes = 128
ends_of = {"field": (2,), "cells": (2, 6), "gradient": (9, 14)}
transfers = (
    ("cells", 1, 1), ("cells", 2, 3), ("gradient", 0, 13), ("gradient", 1, 18), ("gradient", 2, 19),
)
f32, bf16 = jnp.float32, jnp.bfloat16
ANY = pl.BlockSpec(memory_space=pl.ANY)
SMEM = pl.BlockSpec(memory_space=pltpu.SMEM)
params = functools.partial(pltpu.CompilerParams, vmem_limit_bytes=48 * 1024 * 1024)


def split(values):
    high = values.astype(bf16)
    return high, (values - high.astype(f32)).astype(bf16)


def dot(left, right):
    return jnp.dot(left, right, preferred_element_type=f32)


def product(left, right):
    return dot(left[0], right[0]) + (dot(left[0], right[1]) + dot(left[1], right[0]))


def whole(shape):
    return pl.BlockSpec(shape, lambda *_: (0,) * len(shape))


brief = pl.CostEstimate(flops=1, bytes_accessed=1, transcendentals=0)
step_long = pl.CostEstimate(flops=1, bytes_accessed=60_000_000, transcendentals=0)


def fold_rows(values):
    return jnp.sum(values.reshape(-1, 8, values.shape[-1]), axis=0)


def permuted_rows(matrix, bounds, peers):
    rows = matrix.shape[0] // peers
    return jnp.concatenate([matrix[q * rows + low : q * rows + high] for low, high in bounds for q in range(peers)], axis=0)


def field_factors(cholesky_north, cholesky_time, bounds, peers, held_back):
    def kernel(north, time, _, north_high, north_low, time_high, time_low):
        north_high[...], north_low[...] = split(permuted_rows(north[...], bounds, peers))
        time_high[...], time_low[...] = split(time[...].T)

    ny, nt = cholesky_north.shape[0], cholesky_time.shape[0]
    pair = lambda size: [jax.ShapeDtypeStruct((size, size), bf16)] * 2
    full = pl.BlockSpec(memory_space=pltpu.VMEM)
    return pl.pallas_call(
        kernel,
        out_shape=pair(ny) + pair(nt),
        in_specs=[full, full, ANY],
        out_specs=[full] * 4,
        cost_estimate=brief,
        compiler_params=params(),
        name="field_factors",
    )(cholesky_north, cholesky_time, held_back)


def other_factors(layer, cholesky_east, cholesky_north, cholesky_time, bounds, peers, held_back):
    nx = cholesky_east.shape[0]
    span, half = nx // layers, nx // 2
    most = bounds[-1][0] * peers

    def kernel(layer_ref, east, north, time, _, *outs):
        def put(place, values):
            outs[2 * place][...], outs[2 * place + 1][...] = split(values)

        here = layer_ref[0]
        turned = permuted_rows(north[...], bounds, peers).T
        put(0, turned[:, :most])
        put(1, turned[:, most:])
        put(2, time[...])

        @pl.when(here == 1)
        def _():
            put(3, field_scale * east[half:, :half])

        @pl.when(here != 1)
        def _():
            cross = (field_scale * east[half:, :half]).T
            put(3, jnp.concatenate([cross[span:], cross[:span]], axis=0))

        for z in range(layers):

            @pl.when(here == z)
            def _(z=z):
                own = field_scale * east[z * span : (z + 1) * span, z * span : (z + 1) * span]
                put(4, own)
                put(5, own.T)
                if z % 2:
                    put(6, field_scale * east[z * span : (z + 1) * span, (z - 1) * span : z * span])
                else:
                    put(6, (field_scale * east[(z + 1) * span : (z + 2) * span, z * span : (z + 1) * span]).T)

    ny, nt = cholesky_north.shape[0], cholesky_time.shape[0]
    sizes = [(ny, most), (ny, ny - most)] + [(size, size) for size in (nt, half, span, span, span)]
    shapes = [jax.ShapeDtypeStruct(size, bf16) for size in sizes for _ in range(2)]
    outs = pl.pallas_call(
        kernel,
        out_shape=shapes,
        in_specs=[SMEM, whole((nx, nx)), whole((ny, ny)), whole((nt, nt)), ANY],
        out_specs=[whole(s.shape) for s in shapes],
        grid=(1,),
        compiler_params=params(),
        cost_estimate=brief,
        name="other_factors",
    )(layer, cholesky_east, cholesky_north, cholesky_time, held_back)
    return [tuple(outs[2 * i : 2 * i + 2]) for i in range(len(sizes))]


def field(whitened, factors, bounds, peers):
    planes, ny, nt = whitened.shape
    step = 8
    counts = [peers * (high - low) for low, high in bounds]
    parts = nt // lanes

    def kernel(w, north_high, north_low, time_high, time_low, *outs):
        squares = outs[-1]
        north = (north_high[...], north_low[...])
        time = (time_high[...], time_low[...])

        @pl.when(pl.program_id(0) == 0)
        def _():
            squares[...] = jnp.zeros_like(squares)

        def one(x, total):
            values = w[x]
            mixed = product(north, split(product(split(values), time)))
            start = 0
            for out, rows in zip(outs[:-1], counts):
                for h in range(parts):
                    out.reshape(rows * parts * step, lanes)[pl.ds(h * step + x, rows, stride=parts * step), :] = mixed[
                        start : start + rows, h * lanes : (h + 1) * lanes
                    ]
                start += rows
            return total + fold_rows(values * values)

        squares[...] += lax.fori_loop(0, step, one, jnp.zeros((8, nt), f32), unroll=8)

    *groups, squares = pl.pallas_call(
        kernel,
        grid=(planes // step,),
        in_specs=[pl.BlockSpec((step, ny, nt), lambda i: (i, 0, 0))] + [whole(f.shape) for f in factors],
        out_specs=[pl.BlockSpec((rows, parts, step, lanes), lambda i: (0, 0, i, 0)) for rows in counts] + [whole((8, nt))],
        out_shape=[jax.ShapeDtypeStruct((rows, parts, planes, lanes), f32) for rows in counts] + [jax.ShapeDtypeStruct((8, nt), f32)],
        compiler_params=params(),
        cost_estimate=brief,
        name="field",
    )(whitened, *factors)
    return [g.reshape(peers, -1, *g.shape[1:]) for g in groups], squares


def packed(counts, exposure, low, high, peers, *held_back):
    planes, ny, nt = counts.shape
    rows, parts = high - low, nt // lanes
    band = 8 if rows % 8 == 0 and low % 8 == 0 and (ny // peers) % 8 == 0 else rows
    per_peer = ny // peers // band

    def kernel(c, e, *rest):
        out = rest[-1]
        for h in range(parts):
            out[0, 0, h] = c[:, :, h * lanes : (h + 1) * lanes].astype(f32)
            out[0, 1, h] = e[:, :, h * lanes : (h + 1) * lanes].astype(f32)

    source = pl.BlockSpec((planes, band, nt), lambda q, j: (0, q * per_peer + low // band + j, 0))
    return pl.pallas_call(
        kernel,
        grid=(peers, rows // band),
        in_specs=[source, source] + [ANY] * len(held_back),
        out_specs=pl.BlockSpec((1, 2, parts, planes, band, lanes), lambda q, j: (q, 0, 0, 0, j, 0)),
        out_shape=jax.ShapeDtypeStruct((peers, 2, parts, planes, rows, lanes), f32),
        compiler_params=params(),
        cost_estimate=brief,
        name="packed",
    )(counts, exposure, *held_back)


def gate(values, *held_back):
    def kernel(*_):
        pass

    return pl.pallas_call(
        kernel,
        in_specs=[ANY] * (1 + len(held_back)),
        out_specs=ANY,
        out_shape=jax.ShapeDtypeStruct(values.shape, values.dtype),
        input_output_aliases={0: 0},
        cost_estimate=brief,
        name="gate",
    )(values, *held_back)


def lines(*blocks):
    peers = blocks[0].shape[0]
    return jnp.concatenate(
        [jnp.concatenate([b[q, 0, h] for b in blocks for h in range(b.shape[2])], axis=1) for q in range(peers)], axis=0
    )


def put_lines(outs, values):
    outs = outs if isinstance(outs, list) else [outs]
    first = 0
    for out in outs:
        peers, _, parts, planes, width = out.shape
        for q in range(peers):
            for h in range(parts):
                out[q, 0, h] = values[q * planes : (q + 1) * planes, (first + h) * width : (first + h + 1) * width]
        first += parts


def rows_of(array, start):
    peers, _, *rest = array.shape
    return pl.BlockSpec((peers, 1, *rest), lambda y: (0, start + y, 0, 0, 0))


def cross_terms(layer, cross, crossed, own_field, own_residual, rows, *held_back):
    operands = [layer, *cross, *crossed]
    specs = [SMEM, whole(cross[0].shape), whole(cross[1].shape)] + [rows_of(c, 0) for c in crossed]
    pieces = len(crossed)
    for pair in (own_field, own_residual):
        if pair is not None:
            operands.append(pair[0])
            specs.append(rows_of(*pair))
    operands += held_back
    specs += [ANY] * len(held_back)
    peers, _, _, planes, _ = crossed[0].shape
    parts = sum(c.shape[2] for c in crossed)
    span, nt = peers * planes, parts * lanes

    def kernel(layer_ref, high, low, *rest):
        moved, near, far = list(rest[:pieces]), *rest[-2:]
        rest = list(rest[pieces:-2])
        here = layer_ref[0]

        def run(first, second):
            result = product((high[...], low[...]), split(jnp.concatenate([lines(*first), lines(*second)], axis=0)))
            put_lines(near, result[:span])
            put_lines(far, result[span:])

        if own_field is not None:
            own_p = rest.pop(0)

            @pl.when(here == 1)
            def _():
                run(moved, [own_p])

        if own_residual is not None:
            own_r = rest.pop(0)

            @pl.when(here == 2)
            def _():
                run([own_r], moved)

    shape = jax.ShapeDtypeStruct((peers, rows, parts, planes, lanes), f32)
    return pl.pallas_call(
        kernel,
        grid=(rows,),
        in_specs=specs,
        out_specs=[rows_of(shape, 0)] * 2,
        out_shape=[shape] * 2,
        compiler_params=params(),
        cost_estimate=brief,
        name="cross_terms",
    )(*operands)


def cells(layer, factors, moved, near, far, total, own_field, observed, next_field, old_residual, gradient, rows, held_back):
    own, own_t, beside = factors
    peers, _, parts, planes, _ = near.shape
    span, nt = peers * planes, parts * lanes
    pieces = len(moved)
    operands = [layer, *beside, near, far, *moved, *held_back]
    specs = [SMEM, whole((span, span)), whole((span, span)), rows_of(near, 0), rows_of(far, 0)]
    specs += [rows_of(m, 0) for m in moved] + [ANY] * len(held_back)
    shape = jax.ShapeDtypeStruct((peers, rows, parts, planes, lanes), f32)
    shapes, out_specs, aliases = [], [], {}
    names = ["layer", "beside_high", "beside_low", "near", "far"]
    names += ["moved%d" % i for i in range(pieces)] + ["_"] * len(held_back)
    out_names = []

    def take(name, array, spec):
        names.append(name)
        operands.append(array)
        specs.append(spec)

    def give(name, struct, spec):
        out_names.append(name)
        shapes.append(struct)
        out_specs.append(spec)

    if own_field is not None:
        take("own_high", own[0], whole((span, span)))
        take("own_low", own[1], whole((span, span)))
        take("field", own_field[0], rows_of(*own_field))
        table, first = observed
        band = 8 if table.shape[4] % 8 == 0 else table.shape[4]
        take("observed", table, pl.BlockSpec((peers, 2, parts, planes, band, lanes), lambda y: (0, 0, 0, 0, (first + y) // band, 0)))
        take("total", total, whole(total.shape))
        if next_field is not None:
            take("next_field", next_field[0], rows_of(*next_field))
        for i in range(pieces):
            piece = jax.ShapeDtypeStruct((peers, rows, moved[i].shape[2], planes, lanes), f32)
            give("send%d" % i, piece, rows_of(piece, 0))
        give("residual", shape, rows_of(shape, 0))
        give("new_total", jax.ShapeDtypeStruct(total.shape, f32), whole(total.shape))
    if old_residual is not None:
        take("own_t_high", own_t[0], whole((span, span)))
        take("own_t_low", own_t[1], whole((span, span)))
        take("old", old_residual, rows_of(old_residual, 0))
        buffer, high, start = gradient
        struct = jax.ShapeDtypeStruct((peers, high, parts, planes, lanes), f32)
        if buffer is not None:
            aliases[len(operands)] = len(shapes)
            take("buffer", buffer, ANY)
        give("gradient", struct, rows_of(struct, start))

    def kernel(*refs):
        ref = dict(zip(names + out_names, refs))
        here = ref["layer"][0]
        odd, upper = here % 2 == 1, here >= layers // 2
        extra = product((ref["beside_high"][...], ref["beside_low"][...]), split(lines(*[ref["moved%d" % i] for i in range(pieces)])))
        partial = jnp.where((here == 1) | (here == 2), lines(ref["near"]), lines(ref["far"]))
        if own_field is not None:
            log_rate = product((ref["own_high"][...], ref["own_low"][...]), split(lines(ref["field"])))
            log_rate += jnp.where(odd, extra, 0.0) + jnp.where(upper, partial, 0.0)
            row = lax.rem(first + pl.program_id(0), band)
            seen = ref["observed"]

            def pick(kind):
                one = lambda q, h: seen.at[q, kind, h].reshape(planes * band, lanes)[pl.ds(row, planes, stride=band), :]
                return jnp.concatenate([jnp.concatenate([one(q, h) for h in range(parts)], axis=1) for q in range(peers)], axis=0)

            observed_counts = pick(0)
            intensity = pick(1) * jnp.exp(log_rate)
            residual = observed_counts - intensity
            put_lines(ref["residual"], residual)

            @pl.when(pl.program_id(0) == 0)
            def _():
                ref["new_total"][...] = ref["total"][...]

            ref["new_total"][...] += fold_rows(observed_counts * log_rate - intensity)
            send = [ref["send%d" % i] for i in range(pieces)]

            @pl.when(odd)
            def _():
                put_lines(send, residual)

            if next_field is not None:

                @pl.when(jnp.logical_not(odd))
                def _():
                    put_lines(send, lines(ref["next_field"]))

        if old_residual is not None:
            out = product((ref["own_t_high"][...], ref["own_t_low"][...]), split(lines(ref["old"])))
            put_lines(ref["gradient"], out + jnp.where(odd, 0.0, extra) + jnp.where(upper, 0.0, partial))

    outs = pl.pallas_call(
        kernel,
        grid=(rows,),
        in_specs=specs,
        out_specs=out_specs,
        out_shape=shapes,
        input_output_aliases=aliases,
        compiler_params=params(),
        cost_estimate=step_long,
        name="cells",
    )(*operands)
    return dict(zip(out_names, outs))


def finish(groups, partial, north, time, sign):
    planes, ny, nt = partial.shape
    step = 8
    flat = [g.reshape(-1, *g.shape[2:]) for g in groups]
    counts = [g.shape[0] for g in flat]
    parts = nt // lanes

    def pick(refs, x):
        line = lambda ref, rows, h: ref.reshape(rows * parts * step, lanes)[pl.ds(h * step + x, rows, stride=parts * step), :]
        return jnp.concatenate(
            [jnp.concatenate([line(ref, rows, h) for h in range(parts)], axis=1) for ref, rows in zip(refs[:-1], counts)], axis=0
        )

    def kernel(w, north_high, north_low, time_high, time_low, *refs):
        out = refs[-1]
        north_pair = (north_high[...], north_low[...])
        time_pair = (time_high[...], time_low[...])

        if sum(counts) * 2 < ny:
            taken = [pick(refs, x) for x in range(step)]
            timed_high, timed_low = split(product(split(jnp.concatenate(taken, axis=0)), time_pair))
            for x in range(step):
                at = slice(x * sum(counts), (x + 1) * sum(counts))
                out[x] = product(north_pair, (timed_high[at], timed_low[at])) + sign * w[x]
            return

        def one(x, carry):
            out[x] = product(north_pair, split(product(split(pick(refs, x)), time_pair))) + sign * w[x]
            return carry

        lax.fori_loop(0, step, one, 0, unroll=8)

    planes_block = pl.BlockSpec((step, ny, nt), lambda i: (i, 0, 0))
    return pl.pallas_call(
        kernel,
        grid=(planes // step,),
        in_specs=[planes_block]
        + [whole(f.shape) for f in (*north, *time)]
        + [pl.BlockSpec((rows, parts, step, lanes), lambda i: (0, 0, i, 0)) for rows in counts],
        out_specs=planes_block,
        out_shape=jax.ShapeDtypeStruct(partial.shape, f32),
        compiler_params=params(),
        cost_estimate=brief,
        name="finish",
    )(partial, *north, *time, *flat)


def ranges_of(kind, rows, unit):
    unit = unit if kind == "cells" else max(1, rows // chunk_target)
    ends = sorted({min(rows, max(unit, rows * e // 16 // unit * unit)) for e in ends_of[kind]} | {rows})
    return list(zip([0] + ends[:-1], ends))


def per_device(whitened, counts, exposure, cholesky_east, cholesky_north, cholesky_time):
    devices = lax.axis_size("slab")
    peers = devices // layers
    planes, ny, nt = whitened.shape
    rows = ny // peers
    chunk = max(1, rows // chunk_target)
    number = rows // chunk
    unit = 8 if rows % 8 == 0 else rows
    layer = jnp.reshape(lax.axis_index("slab") // peers, (1,)).astype(jnp.int32)
    in_layer = [[z * peers + q for q in range(peers)] for z in range(layers)]

    def exchange(values):
        return lax.all_to_all(values, "slab", 0, 0, tiled=True, axis_index_groups=in_layer)

    def move(values, pairs):
        return lax.ppermute(values, "slab", [(a * peers + q, b * peers + q) for a, b in pairs for q in range(peers)])

    spans = {kind: ranges_of(kind, rows, unit) for kind in ("field", "cells", "gradient")}
    pack = lambda i, *held_back: packed(counts, exposure, *spans["cells"][i], peers, *held_back)
    first = pack(0)
    arrived = {("cells", 0): exchange(first)}
    factors = field_factors(cholesky_north, cholesky_time, spans["field"], peers, first)
    groups, squares = field(whitened, factors, spans["field"], peers)
    start = gate(groups[0], arrived["cells", 0])
    tables = [first, pack(1, start)]
    north, north_last, time, cross, *blocks = other_factors(layer, cholesky_east, cholesky_north, cholesky_time, spans["gradient"], peers, start)
    arrived["field", 0] = gate(exchange(start), *tables[1:], cross[0])

    def sums_over_slab(values):
        if devices & (devices - 1):
            yield lax.psum(values, "slab")
        step = 1
        while step < devices and not devices & (devices - 1):
            values = values + lax.ppermute(values, "slab", [(q, q ^ step) for q in range(devices)])
            yield values
            step *= 2

    def part_of(kind, c):
        i = next(i for i, (low, high) in enumerate(spans[kind]) if low <= c * chunk < high)
        return i, c * chunk - spans[kind][i][0]

    def field_chunk(c):
        i, start = part_of("field", c)
        return arrived["field", i], start

    total = -0.5 * squares
    crossed, residuals, nears, fars = {}, {}, {}, {}
    buffers = {}
    latest = [arrived["field", 0]]

    def do_cross(k, *held_back):
        own_field = field_chunk(k) if k < number else None
        own_residual = (residuals[k - 3], 0) if k >= 3 else None
        near, far = cross_terms(layer, cross, crossed[k - 1], own_field, own_residual, chunk, *held_back)
        forward, backward = k < number, k >= 3
        nears[k + 1] = move(near, [(1, 2)] * forward + [(2, 1)] * backward)
        fars[k + 1] = move(far, [(1, 3)] * forward + [(2, 0)] * backward)
        return near

    def send(kind, i, held_back):
        values = {"field": groups, "cells": tables, "gradient": buffers}[kind][i]
        latest[0] = arrived[kind, i] = exchange(gate(values, *latest, *([] if held_back is None else [held_back])))

    def start_field(k):
        array, start = field_chunk(k + 1)
        values = lax.slice_in_dim(array, start, start + chunk, axis=1)
        crossed[k] = [move(values, [(0, 1), (2, 3)])]
        return values

    start_field(-1)
    send("field", 1, start_field(0))
    near = do_cross(0)
    tables += [pack(i, near) for i in range(2, len(spans["cells"]))]
    start_field(1)
    done = do_cross(1, nears[1], *tables[2:])
    pending = list(transfers)
    for k in range(1, number + 4):
        c, g = k - 1, k - 4
        own_field = observed = next_field = old = gradient = None
        while pending and pending[0][2] * number <= (k - 1) * 16:
            kind, i, _ = pending.pop(0)
            if i < len(spans[kind]):
                send(kind, i, residuals[min(k - 2, number - 1)] if k >= 2 else done)
        if c < number:
            own_field = field_chunk(c)
            i, start = part_of("cells", c)
            observed = (arrived["cells", i], start)
            if k + 2 < number:
                next_field = field_chunk(k + 2)
        if g >= 0:
            old = residuals[g]
            h, start = part_of("gradient", g)
            low, high = spans["gradient"][h]
            gradient = (buffers.get(h), high - low, start)
        held = [done] if k < number + 3 else []
        if k == number + 1:
            sum_steps = sums_over_slab(total)
        if k > number:
            held.append(next(sum_steps))
        outs = cells(layer, blocks, crossed[k - 2], nears[k], fars[k], total, own_field, observed, next_field, old, gradient, chunk, held)
        if c < number:
            residuals[c], total = outs["residual"], outs["new_total"]
        if g >= 0:
            buffers[h] = outs["gradient"]
        if c < number:
            pairs = ([(0, 1), (2, 3)] if k + 2 < number else []) + [(1, 0), (3, 2)]
            crossed[k + 1] = [move(outs["send%d" % i], pairs) for i in range(len(crossed[0]))]
        if k + 1 <= number + 2:
            done = do_cross(k + 1)
    for kind, i, _ in pending:
        if i < len(spans[kind]):
            send(kind, i, None)
    for sums in sum_steps:
        pass
    cell_count = planes * ny * nt * devices
    density = jnp.sum(sums) / cell_count
    *most, last = [arrived["gradient", h] for h in range(len(spans["gradient"]))]
    gradient = finish(most, whitened, north, time, -1.0) if most else whitened
    gradient = finish([last], gradient, north_last, time, 1.0 if most else -1.0)
    return gradient, jnp.reshape(density, (1,))


def solution(mesh):
    placed = P(("chain", "slab"), None, None)
    return jax.shard_map(
        per_device,
        mesh=mesh,
        in_specs=(placed, placed, placed, P(), P(), P()),
        out_specs=(placed, P("chain")),
        check_vma=False,
    )
```

```python
import functools

import jax
import jax.numpy as jnp
from jax import lax
from jax.experimental import pallas as pl
from jax.experimental.pallas import tpu as pltpu
from jax.sharding import PartitionSpec as P

field_scale = 0.6
layers = 4
chunk_target = 16
lanes = 128
ends_of = {"field": (2,), "cells": (2, 6), "gradient": (9, 14)}
transfers = (
    ("cells", 1, 1), ("cells", 2, 3), ("gradient", 0, 13), ("gradient", 1, 18), ("gradient", 2, 19),
)
f32, bf16 = jnp.float32, jnp.bfloat16
ANY = pl.BlockSpec(memory_space=pl.ANY)
SMEM = pl.BlockSpec(memory_space=pltpu.SMEM)
params = functools.partial(pltpu.CompilerParams, vmem_limit_bytes=48 * 1024 * 1024)


def split(values):
    high = values.astype(bf16)
    return high, (values - high.astype(f32)).astype(bf16)


def dot(left, right):
    return jnp.dot(left, right, preferred_element_type=f32)


def product(left, right):
    return dot(left[0], right[0]) + (dot(left[0], right[1]) + dot(left[1], right[0]))


def whole(shape):
    return pl.BlockSpec(shape, lambda *_: (0,) * len(shape))


brief = pl.CostEstimate(flops=1, bytes_accessed=1, transcendentals=0)
step_long = pl.CostEstimate(flops=1, bytes_accessed=60_000_000, transcendentals=0)


def fold_rows(values):
    return jnp.sum(values.reshape(-1, 8, values.shape[-1]), axis=0)


def permuted_rows(matrix, bounds, peers):
    rows = matrix.shape[0] // peers
    return jnp.concatenate([matrix[q * rows + low : q * rows + high] for low, high in bounds for q in range(peers)], axis=0)


def field_factors(cholesky_north, cholesky_time, bounds, peers, held_back):
    def kernel(north, time, _, north_high, north_low, time_high, time_low):
        north_high[...], north_low[...] = split(permuted_rows(north[...], bounds, peers))
        time_high[...], time_low[...] = split(time[...].T)

    ny, nt = cholesky_north.shape[0], cholesky_time.shape[0]
    pair = lambda size: [jax.ShapeDtypeStruct((size, size), bf16)] * 2
    full = pl.BlockSpec(memory_space=pltpu.VMEM)
    return pl.pallas_call(
        kernel,
        out_shape=pair(ny) + pair(nt),
        in_specs=[full, full, ANY],
        out_specs=[full] * 4,
        cost_estimate=brief,
        compiler_params=params(),
        name="field_factors",
    )(cholesky_north, cholesky_time, held_back)


def other_factors(layer, cholesky_east, cholesky_north, cholesky_time, bounds, peers, held_back):
    nx = cholesky_east.shape[0]
    span, half = nx // layers, nx // 2
    most = bounds[-1][0] * peers

    def kernel(layer_ref, east, north, time, _, *outs):
        def put(place, values):
            outs[2 * place][...], outs[2 * place + 1][...] = split(values)

        here = layer_ref[0]
        turned = permuted_rows(north[...], bounds, peers).T
        put(0, turned[:, :most])
        put(1, turned[:, most:])
        put(2, time[...])

        @pl.when(here == 1)
        def _():
            put(3, field_scale * east[half:, :half])

        @pl.when(here != 1)
        def _():
            cross = (field_scale * east[half:, :half]).T
            put(3, jnp.concatenate([cross[span:], cross[:span]], axis=0))

        for z in range(layers):

            @pl.when(here == z)
            def _(z=z):
                own = field_scale * east[z * span : (z + 1) * span, z * span : (z + 1) * span]
                put(4, own)
                put(5, own.T)
                if z % 2:
                    put(6, field_scale * east[z * span : (z + 1) * span, (z - 1) * span : z * span])
                else:
                    put(6, (field_scale * east[(z + 1) * span : (z + 2) * span, z * span : (z + 1) * span]).T)

    ny, nt = cholesky_north.shape[0], cholesky_time.shape[0]
    sizes = [(ny, most), (ny, ny - most)] + [(size, size) for size in (nt, half, span, span, span)]
    shapes = [jax.ShapeDtypeStruct(size, bf16) for size in sizes for _ in range(2)]
    outs = pl.pallas_call(
        kernel,
        out_shape=shapes,
        in_specs=[SMEM, whole((nx, nx)), whole((ny, ny)), whole((nt, nt)), ANY],
        out_specs=[whole(s.shape) for s in shapes],
        grid=(1,),
        compiler_params=params(),
        cost_estimate=brief,
        name="other_factors",
    )(layer, cholesky_east, cholesky_north, cholesky_time, held_back)
    return [tuple(outs[2 * i : 2 * i + 2]) for i in range(len(sizes))]


def field(whitened, factors, bounds, peers):
    planes, ny, nt = whitened.shape
    step = 8
    counts = [peers * (high - low) for low, high in bounds]
    parts = nt // lanes

    def kernel(w, north_high, north_low, time_high, time_low, *outs):
        squares = outs[-1]
        north = (north_high[...], north_low[...])
        time = (time_high[...], time_low[...])

        @pl.when(pl.program_id(0) == 0)
        def _():
            squares[...] = jnp.zeros_like(squares)

        def one(x, total):
            values = w[x]
            mixed = product(north, split(product(split(values), time)))
            start = 0
            for out, rows in zip(outs[:-1], counts):
                for h in range(parts):
                    out.reshape(rows * parts * step, lanes)[pl.ds(h * step + x, rows, stride=parts * step), :] = mixed[
                        start : start + rows, h * lanes : (h + 1) * lanes
                    ]
                start += rows
            return total + fold_rows(values * values)

        squares[...] += lax.fori_loop(0, step, one, jnp.zeros((8, nt), f32), unroll=8)

    *groups, squares = pl.pallas_call(
        kernel,
        grid=(planes // step,),
        in_specs=[pl.BlockSpec((step, ny, nt), lambda i: (i, 0, 0))] + [whole(f.shape) for f in factors],
        out_specs=[pl.BlockSpec((rows, parts, step, lanes), lambda i: (0, 0, i, 0)) for rows in counts] + [whole((8, nt))],
        out_shape=[jax.ShapeDtypeStruct((rows, parts, planes, lanes), f32) for rows in counts] + [jax.ShapeDtypeStruct((8, nt), f32)],
        compiler_params=params(),
        cost_estimate=brief,
        name="field",
    )(whitened, *factors)
    return [g.reshape(peers, -1, *g.shape[1:]) for g in groups], squares


def packed(counts, exposure, low, high, peers, *held_back):
    planes, ny, nt = counts.shape
    rows, parts = high - low, nt // lanes
    band = 8 if rows % 8 == 0 and low % 8 == 0 and (ny // peers) % 8 == 0 else rows
    per_peer = ny // peers // band

    def kernel(c, e, *rest):
        out = rest[-1]
        for h in range(parts):
            out[0, 0, h] = c[:, :, h * lanes : (h + 1) * lanes].astype(f32)
            out[0, 1, h] = e[:, :, h * lanes : (h + 1) * lanes].astype(f32)

    source = pl.BlockSpec((planes, band, nt), lambda q, j: (0, q * per_peer + low // band + j, 0))
    return pl.pallas_call(
        kernel,
        grid=(peers, rows // band),
        in_specs=[source, source] + [ANY] * len(held_back),
        out_specs=pl.BlockSpec((1, 2, parts, planes, band, lanes), lambda q, j: (q, 0, 0, 0, j, 0)),
        out_shape=jax.ShapeDtypeStruct((peers, 2, parts, planes, rows, lanes), f32),
        compiler_params=params(),
        cost_estimate=brief,
        name="packed",
    )(counts, exposure, *held_back)


def gate(values, *held_back):
    def kernel(*_):
        pass

    return pl.pallas_call(
        kernel,
        in_specs=[ANY] * (1 + len(held_back)),
        out_specs=ANY,
        out_shape=jax.ShapeDtypeStruct(values.shape, values.dtype),
        input_output_aliases={0: 0},
        cost_estimate=brief,
        name="gate",
    )(values, *held_back)


def lines(*blocks):
    peers = blocks[0].shape[0]
    return jnp.concatenate(
        [jnp.concatenate([b[q, 0, h] for b in blocks for h in range(b.shape[2])], axis=1) for q in range(peers)], axis=0
    )


def put_lines(outs, values):
    outs = outs if isinstance(outs, list) else [outs]
    first = 0
    for out in outs:
        peers, _, parts, planes, width = out.shape
        for q in range(peers):
            for h in range(parts):
                out[q, 0, h] = values[q * planes : (q + 1) * planes, (first + h) * width : (first + h + 1) * width]
        first += parts


def rows_of(array, start):
    peers, _, *rest = array.shape
    return pl.BlockSpec((peers, 1, *rest), lambda y: (0, start + y, 0, 0, 0))


def cross_terms(layer, cross, crossed, own_field, own_residual, rows, *held_back):
    operands = [layer, *cross, *crossed]
    specs = [SMEM, whole(cross[0].shape), whole(cross[1].shape)] + [rows_of(c, 0) for c in crossed]
    pieces = len(crossed)
    for pair in (own_field, own_residual):
        if pair is not None:
            operands.append(pair[0])
            specs.append(rows_of(*pair))
    operands += held_back
    specs += [ANY] * len(held_back)
    peers, _, _, planes, _ = crossed[0].shape
    parts = sum(c.shape[2] for c in crossed)
    span, nt = peers * planes, parts * lanes

    def kernel(layer_ref, high, low, *rest):
        moved, near, far = list(rest[:pieces]), *rest[-2:]
        rest = list(rest[pieces:-2])
        here = layer_ref[0]

        def run(first, second):
            result = product((high[...], low[...]), split(jnp.concatenate([lines(*first), lines(*second)], axis=0)))
            put_lines(near, result[:span])
            put_lines(far, result[span:])

        if own_field is not None:
            own_p = rest.pop(0)

            @pl.when(here == 1)
            def _():
                run(moved, [own_p])

        if own_residual is not None:
            own_r = rest.pop(0)

            @pl.when(here == 2)
            def _():
                run([own_r], moved)

    shape = jax.ShapeDtypeStruct((peers, rows, parts, planes, lanes), f32)
    return pl.pallas_call(
        kernel,
        grid=(rows,),
        in_specs=specs,
        out_specs=[rows_of(shape, 0)] * 2,
        out_shape=[shape] * 2,
        compiler_params=params(),
        cost_estimate=brief,
        name="cross_terms",
    )(*operands)


def cells(layer, factors, moved, near, far, total, own_field, observed, next_field, old_residual, gradient, rows, held_back):
    own, own_t, beside = factors
    peers, _, parts, planes, _ = near.shape
    span, nt = peers * planes, parts * lanes
    pieces = len(moved)
    operands = [layer, *beside, near, far, *moved, *held_back]
    specs = [SMEM, whole((span, span)), whole((span, span)), rows_of(near, 0), rows_of(far, 0)]
    specs += [rows_of(m, 0) for m in moved] + [ANY] * len(held_back)
    shape = jax.ShapeDtypeStruct((peers, rows, parts, planes, lanes), f32)
    shapes, out_specs, aliases = [], [], {}
    names = ["layer", "beside_high", "beside_low", "near", "far"]
    names += ["moved%d" % i for i in range(pieces)] + ["_"] * len(held_back)
    out_names = []

    def take(name, array, spec):
        names.append(name)
        operands.append(array)
        specs.append(spec)

    def give(name, struct, spec):
        out_names.append(name)
        shapes.append(struct)
        out_specs.append(spec)

    if own_field is not None:
        take("own_high", own[0], whole((span, span)))
        take("own_low", own[1], whole((span, span)))
        take("field", own_field[0], rows_of(*own_field))
        table, first = observed
        band = 8 if table.shape[4] % 8 == 0 else table.shape[4]
        take("observed", table, pl.BlockSpec((peers, 2, parts, planes, band, lanes), lambda y: (0, 0, 0, 0, (first + y) // band, 0)))
        take("total", total, whole(total.shape))
        if next_field is not None:
            take("next_field", next_field[0], rows_of(*next_field))
        for i in range(pieces):
            piece = jax.ShapeDtypeStruct((peers, rows, moved[i].shape[2], planes, lanes), f32)
            give("send%d" % i, piece, rows_of(piece, 0))
        give("residual", shape, rows_of(shape, 0))
        give("new_total", jax.ShapeDtypeStruct(total.shape, f32), whole(total.shape))
    if old_residual is not None:
        take("own_t_high", own_t[0], whole((span, span)))
        take("own_t_low", own_t[1], whole((span, span)))
        take("old", old_residual, rows_of(old_residual, 0))
        buffer, high, start = gradient
        struct = jax.ShapeDtypeStruct((peers, high, parts, planes, lanes), f32)
        if buffer is not None:
            aliases[len(operands)] = len(shapes)
            take("buffer", buffer, ANY)
        give("gradient", struct, rows_of(struct, start))

    def kernel(*refs):
        ref = dict(zip(names + out_names, refs))
        here = ref["layer"][0]
        odd, upper = here % 2 == 1, here >= layers // 2
        extra = product((ref["beside_high"][...], ref["beside_low"][...]), split(lines(*[ref["moved%d" % i] for i in range(pieces)])))
        partial = jnp.where((here == 1) | (here == 2), lines(ref["near"]), lines(ref["far"]))
        if own_field is not None:
            log_rate = product((ref["own_high"][...], ref["own_low"][...]), split(lines(ref["field"])))
            log_rate += jnp.where(odd, extra, 0.0) + jnp.where(upper, partial, 0.0)
            row = lax.rem(first + pl.program_id(0), band)
            seen = ref["observed"]

            def pick(kind):
                one = lambda q, h: seen.at[q, kind, h].reshape(planes * band, lanes)[pl.ds(row, planes, stride=band), :]
                return jnp.concatenate([jnp.concatenate([one(q, h) for h in range(parts)], axis=1) for q in range(peers)], axis=0)

            observed_counts = pick(0)
            intensity = pick(1) * jnp.exp(log_rate)
            residual = observed_counts - intensity
            put_lines(ref["residual"], residual)

            @pl.when(pl.program_id(0) == 0)
            def _():
                ref["new_total"][...] = ref["total"][...]

            ref["new_total"][...] += fold_rows(observed_counts * log_rate - intensity)
            send = [ref["send%d" % i] for i in range(pieces)]

            @pl.when(odd)
            def _():
                put_lines(send, residual)

            if next_field is not None:

                @pl.when(jnp.logical_not(odd))
                def _():
                    put_lines(send, lines(ref["next_field"]))

        if old_residual is not None:
            out = product((ref["own_t_high"][...], ref["own_t_low"][...]), split(lines(ref["old"])))
            put_lines(ref["gradient"], out + jnp.where(odd, 0.0, extra) + jnp.where(upper, 0.0, partial))

    outs = pl.pallas_call(
        kernel,
        grid=(rows,),
        in_specs=specs,
        out_specs=out_specs,
        out_shape=shapes,
        input_output_aliases=aliases,
        compiler_params=params(),
        cost_estimate=step_long,
        name="cells",
    )(*operands)
    return dict(zip(out_names, outs))


def finish(groups, partial, north, time, sign):
    planes, ny, nt = partial.shape
    step = 8
    flat = [g.reshape(-1, *g.shape[2:]) for g in groups]
    counts = [g.shape[0] for g in flat]
    parts = nt // lanes

    def pick(refs, x):
        line = lambda ref, rows, h: ref.reshape(rows * parts * step, lanes)[pl.ds(h * step + x, rows, stride=parts * step), :]
        return jnp.concatenate(
            [jnp.concatenate([line(ref, rows, h) for h in range(parts)], axis=1) for ref, rows in zip(refs[:-1], counts)], axis=0
        )

    def kernel(w, north_high, north_low, time_high, time_low, *refs):
        out = refs[-1]
        north_pair = (north_high[...], north_low[...])
        time_pair = (time_high[...], time_low[...])

        if sum(counts) * 2 < ny:
            taken = [pick(refs, x) for x in range(step)]
            timed_high, timed_low = split(product(split(jnp.concatenate(taken, axis=0)), time_pair))
            for x in range(step):
                at = slice(x * sum(counts), (x + 1) * sum(counts))
                out[x] = product(north_pair, (timed_high[at], timed_low[at])) + sign * w[x]
            return

        def one(x, carry):
            out[x] = product(north_pair, split(product(split(pick(refs, x)), time_pair))) + sign * w[x]
            return carry

        lax.fori_loop(0, step, one, 0, unroll=8)

    planes_block = pl.BlockSpec((step, ny, nt), lambda i: (i, 0, 0))
    return pl.pallas_call(
        kernel,
        grid=(planes // step,),
        in_specs=[planes_block]
        + [whole(f.shape) for f in (*north, *time)]
        + [pl.BlockSpec((rows, parts, step, lanes), lambda i: (0, 0, i, 0)) for rows in counts],
        out_specs=planes_block,
        out_shape=jax.ShapeDtypeStruct(partial.shape, f32),
        compiler_params=params(),
        cost_estimate=brief,
        name="finish",
    )(partial, *north, *time, *flat)


def ranges_of(kind, rows, unit):
    unit = unit if kind == "cells" else max(1, rows // chunk_target)
    ends = sorted({min(rows, max(unit, rows * e // 16 // unit * unit)) for e in ends_of[kind]} | {rows})
    return list(zip([0] + ends[:-1], ends))


def per_device(whitened, counts, exposure, cholesky_east, cholesky_north, cholesky_time):
    devices = lax.axis_size("slab")
    peers = devices // layers
    planes, ny, nt = whitened.shape
    rows = ny // peers
    chunk = max(1, rows // chunk_target)
    number = rows // chunk
    unit = 8 if rows % 8 == 0 else rows
    layer = jnp.reshape(lax.axis_index("slab") // peers, (1,)).astype(jnp.int32)
    in_layer = [[z * peers + q for q in range(peers)] for z in range(layers)]

    def exchange(values):
        return lax.all_to_all(values, "slab", 0, 0, tiled=True, axis_index_groups=in_layer)

    def move(values, pairs):
        return lax.ppermute(values, "slab", [(a * peers + q, b * peers + q) for a, b in pairs for q in range(peers)])

    spans = {kind: ranges_of(kind, rows, unit) for kind in ("field", "cells", "gradient")}
    pack = lambda i, *held_back: packed(counts, exposure, *spans["cells"][i], peers, *held_back)
    first = pack(0)
    arrived = {("cells", 0): exchange(first)}
    factors = field_factors(cholesky_north, cholesky_time, spans["field"], peers, first)
    groups, squares = field(whitened, factors, spans["field"], peers)
    start = gate(groups[0], arrived["cells", 0])
    tables = [first, pack(1, start)]
    north, north_last, time, cross, *blocks = other_factors(layer, cholesky_east, cholesky_north, cholesky_time, spans["gradient"], peers, start)
    arrived["field", 0] = gate(exchange(start), *tables[1:], cross[0])

    def sums_over_slab(values):
        if devices & (devices - 1):
            yield lax.psum(values, "slab")
        else:
            steps = [1 << bit for bit in range(devices.bit_length() - 1)]
            for step in steps[1:] + steps[:1]:
                values = values + lax.ppermute(values, "slab", [(q, q ^ step) for q in range(devices)])
                yield values

    def part_of(kind, c):
        i = next(i for i, (low, high) in enumerate(spans[kind]) if low <= c * chunk < high)
        return i, c * chunk - spans[kind][i][0]

    def field_chunk(c):
        i, start = part_of("field", c)
        return arrived["field", i], start

    total = -0.5 * squares
    crossed, residuals, nears, fars = {}, {}, {}, {}
    buffers = {}
    latest = [arrived["field", 0]]

    def do_cross(k, *held_back):
        own_field = field_chunk(k) if k < number else None
        own_residual = (residuals[k - 3], 0) if k >= 3 else None
        near, far = cross_terms(layer, cross, crossed[k - 1], own_field, own_residual, chunk, *held_back)
        forward, backward = k < number, k >= 3
        nears[k + 1] = move(near, [(1, 2)] * forward + [(2, 1)] * backward)
        fars[k + 1] = move(far, [(1, 3)] * forward + [(2, 0)] * backward)
        return near

    def send(kind, i, held_back):
        values = {"field": groups, "cells": tables, "gradient": buffers}[kind][i]
        latest[0] = arrived[kind, i] = exchange(gate(values, *latest, *([] if held_back is None else [held_back])))

    def start_field(k):
        array, start = field_chunk(k + 1)
        values = lax.slice_in_dim(array, start, start + chunk, axis=1)
        crossed[k] = [move(values, [(0, 1), (2, 3)])]
        return values

    start_field(-1)
    send("field", 1, start_field(0))
    near = do_cross(0)
    tables += [pack(i, near) for i in range(2, len(spans["cells"]))]
    start_field(1)
    done = do_cross(1, nears[1], *tables[2:])
    pending = list(transfers)
    for k in range(1, number + 4):
        c, g = k - 1, k - 4
        own_field = observed = next_field = old = gradient = None
        while pending and pending[0][2] * number <= (k - 1) * 16:
            kind, i, _ = pending.pop(0)
            if i < len(spans[kind]):
                send(kind, i, residuals[min(k - 2, number - 1)] if k >= 2 else done)
        if c < number:
            own_field = field_chunk(c)
            i, start = part_of("cells", c)
            observed = (arrived["cells", i], start)
            if k + 2 < number:
                next_field = field_chunk(k + 2)
        if g >= 0:
            old = residuals[g]
            h, start = part_of("gradient", g)
            low, high = spans["gradient"][h]
            gradient = (buffers.get(h), high - low, start)
        held = [done] if k < number + 3 else []
        if k == number + 1:
            sum_steps = sums_over_slab(total)
        if k > number:
            held.append(next(sum_steps))
        outs = cells(layer, blocks, crossed[k - 2], nears[k], fars[k], total, own_field, observed, next_field, old, gradient, chunk, held)
        if c < number:
            residuals[c], total = outs["residual"], outs["new_total"]
        if g >= 0:
            buffers[h] = outs["gradient"]
        if c < number:
            pairs = ([(0, 1), (2, 3)] if k + 2 < number else []) + [(1, 0), (3, 2)]
            crossed[k + 1] = [move(outs["send%d" % i], pairs) for i in range(len(crossed[0]))]
        if k + 1 <= number + 2:
            done = do_cross(k + 1)
    for kind, i, _ in pending:
        if i < len(spans[kind]):
            send(kind, i, None)
    for sums in sum_steps:
        pass
    cell_count = planes * ny * nt * devices
    density = jnp.sum(sums) / cell_count
    *most, last = [arrived["gradient", h] for h in range(len(spans["gradient"]))]
    gradient = finish(most, whitened, north, time, -1.0) if most else whitened
    gradient = finish([last], gradient, north_last, time, 1.0 if most else -1.0)
    return gradient, jnp.reshape(density, (1,))


def solution(mesh):
    placed = P(("chain", "slab"), None, None)
    return jax.shard_map(
        per_device,
        mesh=mesh,
        in_specs=(placed, placed, placed, P(), P(), P()),
        out_specs=(placed, P("chain")),
        check_vma=False,
    )
```
